32 devices in a mesh: groups: 2 (over y), node: 2 (over x), local: 4 (over z), rep: 2 (over core).
Axes of the slice: x: 2, y: 2, z: 4, core: 2. Of those that a mesh axis runs over, the one named last changes fastest.
Arguments:
- tokens: bfloat16 [4096, 3584], P(('groups', 'node', 'local', 'rep')), parts along dimension 0, may hold values from -6 to 6
- cotangent: bfloat16 [4096, 3584], P(('groups', 'node', 'local', 'rep')), parts along dimension 0, may hold values from -6 to 6
- expert_ids: int32 [4096, 1], P(('groups', 'node', 'local', 'rep')), parts along dimension 0, may hold values from 0 to 1
- gate_values: float32 [4096, 1], P(('groups', 'node', 'local', 'rep')), parts along dimension 0, may hold values from 0.1 to 1
- w_gate: bfloat16 [2, 3584, 1024], P('node', 'local', 'rep'), may hold values from -0.09375 to 0.09375
- w_up: bfloat16 [2, 3584, 1024], P('node', 'local', 'rep'), may hold values from -0.09375 to 0.09375
- feedback: bfloat16 [2, 1024, 3584], P('node', 'rep', 'local'), may hold values from -8 to 8
Outputs:
- grad_down: bfloat16 [4, 1024, 3584], P(('groups', 'node'), 'rep', 'local'), parts along dimension 0
The draws below stay inside these ranges and needn't reach their ends.
There are 2 independent parts, one for each index of `groups`. The reference program is written for one: setup_inputs(seed, part) draws one part's arguments, and reference() takes and returns one part's arrays. A program takes and returns all parts, laid end to end along the dimension named above; an argument that names none is the same for every part. Nothing has to cross between parts.
All inputs are finite; a program needn't handle non-finite values.
Results may differ from the reference program's by a relative error of at most 0.012.
Values may be sent and summed in bfloat16 or wider, within the bound.
No kernel may reach another device: no remote copies, remote signals or barrier semaphores. Data moves between devices by JAX's collectives and lax.ppermute only.
A program may use at most 64 MiB of HBM per device.

```python
import math
import jax
import jax.numpy as jnp
from jax import lax

D = 3584
HID = 1024
TOPK = 1
T_DEV = 128
TOKENS = 2048
EXPERTS = 2
CAP = 64
N_NODE = 2
N_LOCAL = 4
N_REP = 2


def shard_levels(key, shape, split, least, largest):
    loudness, own = 1.0, jax.random.fold_in(key, 6)
    for dim, blocks in split:
        heights = jnp.exp(jax.random.uniform(jax.random.fold_in(own, dim), (blocks,), jnp.float32, least / len(split), largest / len(split)))
        loudness = loudness * jnp.repeat(heights, shape[dim] // blocks).reshape([-1 if axis == dim else 1 for axis in range(len(shape))])
    return loudness


def choose_distinct(stream_key, rows, count, top, lift):
    order = jax.random.permutation(jax.random.fold_in(stream_key, 1), count)
    favour = order
    for power in range(3):
        favour = favour * favour // count
    favour = favour * lift // count
    tickets = jax.random.randint(jax.random.fold_in(stream_key, 2), (rows, count), 0, 4096) + favour
    fixed_rows = jax.random.permutation(jax.random.fold_in(stream_key, 3), rows)[jnp.arange(count) % rows]
    tickets = jnp.where(jnp.arange(rows)[:, None] == fixed_rows[None, :], 1 << 14, tickets)
    priority = tickets * count + jnp.arange(count)
    return lax.top_k(priority.astype(jnp.int32), top)[1].astype(jnp.int32)


def scatter_about(own_key, shape, scale, reach, split=(), held_as=jnp.bfloat16):
    result = jax.random.normal(own_key, shape, jnp.float32) * scale
    if len(split) > 0:
        result = shard_levels(own_key, shape, split, -0.22, 0.18) * result
    return jnp.clip(result, min=-reach, max=reach).astype(held_as)


def setup_inputs(seed: int = 0, part: int = 0) -> dict:
    seeds = jax.random.split(jax.random.key(seed), 8)
    own_keys = jax.random.split(jax.random.fold_in(seeds[7], part), 8)
    return {
        "tokens": scatter_about(own_keys[0], (TOKENS, D), 1.0, 6.0, ((0, 16),)),
        "cotangent": scatter_about(own_keys[1], (TOKENS, D), 1.0, 6.0, ((0, 16),)),
        "expert_ids": choose_distinct(own_keys[2], TOKENS, EXPERTS, TOPK, 8192),
        "gate_values": jnp.clip(jnp.exp(math.log(1.0) - 2.3025851 * jax.random.uniform(own_keys[3], (TOKENS, TOPK), jnp.float32) ** shard_levels(own_keys[3], (TOKENS, TOPK), ((0, 16),), -0.2, 0.2)), 0.1, 1.0),
        "w_gate": scatter_about(seeds[4], (EXPERTS, D, HID), D ** -0.5, 0.09375, ((0, 2), (1, 4), (2, 2))),
        "w_up": scatter_about(seeds[5], (EXPERTS, D, HID), D ** -0.5, 0.09375, ((0, 2), (1, 4), (2, 2))),
        "feedback": scatter_about(seeds[6], (EXPERTS, HID, D), 2.0, 8.0, ((0, 2), (1, 2), (2, 4))),
    }


def reference(tokens, cotangent, expert_ids, gate_values, w_gate, w_up, feedback):
    sources = TOKENS // T_DEV
    per_block = T_DEV * TOPK
    flat_ids = expert_ids.reshape(sources, per_block)
    onehot = (flat_ids[:, :, None] == jnp.arange(EXPERTS, dtype=jnp.int32)[None, None, :]).astype(jnp.int32)
    before = jnp.cumsum(onehot, axis=1) - onehot
    slot_rank = lax.optimization_barrier(jnp.sum(before * onehot, axis=2)).astype(jnp.int32)
    pair_index = jnp.arange(TOKENS * TOPK, dtype=jnp.int32).reshape(sources, per_block)
    source_index = jnp.broadcast_to(jnp.arange(sources, dtype=jnp.int32)[:, None], (sources, per_block))
    target = jnp.where(slot_rank < CAP, flat_ids, EXPERTS).astype(jnp.int32)
    table = jnp.full((EXPERTS, sources, CAP), TOKENS * TOPK, jnp.int32)
    table = table.at[target, source_index, jnp.minimum(slot_rank, CAP - 1)].set(pair_index, mode='drop')
    tokens_pad = jnp.concatenate([tokens, jnp.zeros((1, D), jnp.bfloat16)], axis=0)
    cot_pad = jnp.concatenate([cotangent, jnp.zeros((1, D), jnp.bfloat16)], axis=0)
    gate_pad = jnp.concatenate([gate_values.reshape(-1), jnp.zeros((1,), jnp.float32)], axis=0)

    def expert_grad(inputs):
        entries, gate_w, up_w, residual = inputs
        pair_flat = entries.reshape(-1)
        token_row = (pair_flat // TOPK).astype(jnp.int32)
        x_rows = tokens_pad[token_row]
        scaled = (gate_pad[pair_flat][:, None] * cot_pad[token_row].astype(jnp.float32)).astype(jnp.bfloat16)
        pre_gate = jnp.dot(x_rows, gate_w, preferred_element_type=jnp.float32)
        pre_up = jnp.dot(x_rows, up_w, preferred_element_type=jnp.float32)
        hidden = (jax.nn.silu(pre_gate) * pre_up).astype(jnp.bfloat16)
        hidden_split = hidden.reshape(N_NODE, N_LOCAL, N_REP, CAP, HID).astype(jnp.float32)
        scaled_split = scaled.reshape(N_NODE, N_LOCAL, N_REP, CAP, D).astype(jnp.float32)
        term_grad = jnp.einsum('nlrch,nlrcd->lhd', hidden_split, scaled_split)
        compressed = lax.optimization_barrier(term_grad.astype(jnp.bfloat16)).astype(jnp.float32)
        total = lax.optimization_barrier(jnp.sum(compressed, axis=0)) + residual.astype(jnp.float32)
        return total.astype(jnp.bfloat16)
    return lax.map(expert_grad, (table, w_gate, w_up, feedback))
```

```python
import functools

import jax
import jax.numpy as jnp
from jax import lax
from jax.experimental import pallas as pl
from jax.experimental.pallas import tpu as pltpu
from jax.sharding import PartitionSpec as P


def swapped(value, axis):
    return lax.ppermute(value, axis, [(s, s ^ 1) for s in range(lax.axis_size(axis))])


def dispatch_kernel(nodes, blocks, capacity, ids_ref, gate_ref, x_ref, c_ref, sx_ref, sy_ref):
    pairs = ids_ref.shape[1]
    width = x_ref.shape[1] // blocks
    ids = ids_ref[...]
    row = lax.broadcasted_iota(jnp.int32, (pairs, pairs), 0)
    col = lax.broadcasted_iota(jnp.int32, (pairs, pairs), 1)
    earlier = (row < col).astype(jnp.bfloat16)
    slots = lax.broadcasted_iota(jnp.int32, (capacity, pairs), 0)
    for node in range(nodes):
        named = ids == node
        rank = jnp.dot(
            jnp.broadcast_to(named, (8, pairs)).astype(jnp.bfloat16),
            earlier,
            preferred_element_type=jnp.float32,
        )[:1].astype(jnp.int32)
        pick = jnp.where((rank == slots) & named, 1.0, 0.0)
        gate = jnp.sum(pick * gate_ref[...], axis=1, keepdims=True)
        pick = pick.astype(jnp.bfloat16)
        for block in range(blocks):
            cols = slice(block * width, (block + 1) * width)
            x_rows = jnp.dot(pick, x_ref[:, cols], preferred_element_type=jnp.float32)
            c_rows = jnp.dot(pick, c_ref[:, cols], preferred_element_type=jnp.float32)
            sx_ref[node * blocks + block] = x_rows.astype(jnp.bfloat16)
            sy_ref[node * blocks + block] = (gate * c_rows).astype(jnp.bfloat16)


def dispatch(ids, gates, tokens, cotangent, nodes, blocks, capacity):
    width = tokens.shape[1] // blocks
    out = jax.ShapeDtypeStruct((nodes * blocks, capacity, width), jnp.bfloat16)
    vmem = pl.BlockSpec(memory_space=pltpu.VMEM)
    return pl.pallas_call(
        functools.partial(dispatch_kernel, nodes, blocks, capacity),
        out_shape=(out, out),
        in_specs=[vmem] * 4,
        out_specs=(vmem, vmem),
        compiler_params=pltpu.CompilerParams(vmem_limit_bytes=32 << 20),
    )(ids, gates, tokens, cotangent)


def local(tokens, cotangent, expert_ids, gate_values, w_gate, w_up, feedback):
    token_count = tokens.shape[0]
    top_count = expert_ids.shape[1]
    nodes, blocks = lax.axis_size("node"), lax.axis_size("local")
    capacity = max(2, token_count * top_count // nodes)
    width = tokens.shape[1] // blocks
    if top_count > 1:
        tokens = jnp.repeat(tokens, top_count, axis=0)
        cotangent = jnp.repeat(cotangent, top_count, axis=0)
    send_x, send_y = dispatch(
        expert_ids.reshape(1, -1),
        gate_values.reshape(1, -1),
        tokens,
        cotangent,
        nodes,
        blocks,
        capacity,
    )
    axes = ("node", "local")
    own_x = lax.all_to_all(send_x, axes, 0, 0, tiled=True).reshape(-1, width)
    own_y = lax.all_to_all(send_y, axes, 0, 0, tiled=True).reshape(-1, width)
    x_rows = jnp.concatenate([own_x, swapped(own_x, "rep")], axis=0)
    y_rows = jnp.concatenate([own_y, swapped(own_y, "rep")], axis=0)
    weights = jnp.concatenate([w_gate[0], w_up[0]], axis=1)
    partial = jnp.dot(x_rows, weights, preferred_element_type=jnp.float32).astype(jnp.bfloat16)
    pre = lax.psum_scatter(partial, "local", scatter_dimension=0, tiled=True).astype(jnp.float32)
    pre_gate, pre_up = jnp.split(pre, 2, axis=1)
    hidden = (jax.nn.silu(pre_gate) * pre_up).astype(jnp.bfloat16)
    hidden = lax.all_gather(hidden, "local", axis=0, tiled=True)
    grad = lax.dot_general(
        hidden, y_rows, (((0,), (0,)), ((), ())), preferred_element_type=jnp.float32
    )
    return (grad + feedback[0].astype(jnp.float32)).astype(jnp.bfloat16)[None]


def solution(mesh):
    rows = P(("groups", "node", "local", "rep"), None)
    weights = P("node", "local", "rep")
    return jax.shard_map(
        local,
        mesh=mesh,
        in_specs=(rows, rows, rows, rows, weights, weights, P("node", "rep", "local")),
        out_specs=P(("groups", "node"), "rep", "local"),
        check_vma=False,
    )
```

```python
import functools

import jax
import jax.numpy as jnp
from jax import lax
from jax.experimental import pallas as pl
from jax.experimental.pallas import tpu as pltpu
from jax.sharding import Mesh
from jax.sharding import PartitionSpec as P

KERNEL = pltpu.CompilerParams(vmem_limit_bytes=40 << 20)
SMEM = pl.BlockSpec(memory_space=pltpu.SMEM)
WHOLE = pl.BlockSpec()


def swapped(value, axis, distance=1):
    pairs = [(s, s ^ distance) for s in range(lax.axis_size(axis))]
    return lax.ppermute(value, axis, pairs)


def dispatch_kernel(nodes, side, capacity, half_ref, ids_ref, gate_ref, x_ref, c_ref, sx_ref, sy_ref):
    pairs = ids_ref.shape[1]
    width = sx_ref.shape[-1]
    half = half_ref[0]
    ids = ids_ref[...]
    row = lax.broadcasted_iota(jnp.int32, (pairs, pairs), 0)
    col = lax.broadcasted_iota(jnp.int32, (pairs, pairs), 1)
    earlier = (row < col).astype(jnp.bfloat16)
    slots = lax.broadcasted_iota(jnp.int32, (capacity, pairs), 0)
    for node in range(nodes):
        named = ids == node
        rank = jnp.dot(
            jnp.broadcast_to(jnp.where(named, 1.0, 0.0), (8, pairs)).astype(jnp.bfloat16),
            earlier,
            preferred_element_type=jnp.float32,
        )[:1].astype(jnp.int32)
        pick = jnp.where((rank == slots) & named, 1.0, 0.0)
        gate = jnp.sum(pick * gate_ref[...], axis=1, keepdims=True)
        pick = pick.astype(jnp.bfloat16)
        for hi in range(2):
            for lo in range(side):
                block = hi * side + lo
                cols = slice(block * width, (block + 1) * width)
                x_rows = jnp.dot(pick, x_ref[:, cols], preferred_element_type=jnp.float32)
                c_rows = jnp.dot(pick, c_ref[:, cols], preferred_element_type=jnp.float32)
                sx_ref[node * side + lo, half ^ hi] = x_rows.astype(jnp.bfloat16)
                sy_ref[(hi * nodes + node) * side + lo] = (gate * c_rows).astype(jnp.bfloat16)


def dispatch(half, ids, gates, tokens, cotangent, nodes, side, capacity):
    width = tokens.shape[1] // (2 * side)
    return pl.pallas_call(
        functools.partial(dispatch_kernel, nodes, side, capacity),
        out_shape=(
            jax.ShapeDtypeStruct((nodes * side, 2, capacity, width), jnp.bfloat16),
            jax.ShapeDtypeStruct((2 * nodes * side, capacity, width), jnp.bfloat16),
        ),
        in_specs=[SMEM] + [WHOLE] * 4,
        out_specs=(WHOLE, WHOLE),
        compiler_params=KERNEL,
    )(half, ids, gates, tokens, cotangent)


def row_chunk(own_ref, other_ref, index, quarter, side):
    per_core = side // 2
    count = own_ref.shape[0] // per_core
    place = index % per_core
    own = own_ref[pl.ds(place * count, count), quarter]
    other = other_ref[pl.ds(place * count, count), quarter]
    rows = jnp.where(index < per_core, own, other)
    return rows.reshape(-1, rows.shape[-1])


def first_kernel(side, lo_ref, own_ref, other_ref, gate_ref, up_ref, acc_ref):
    hidden = gate_ref.shape[-1]
    for step in range(side):
        x = row_chunk(own_ref, other_ref, lo_ref[0] ^ step, 0, side)
        acc_ref[step, :, :hidden] = jnp.dot(x, gate_ref[...], preferred_element_type=jnp.float32)
        acc_ref[step, :, hidden:] = jnp.dot(x, up_ref[...], preferred_element_type=jnp.float32)


def second_kernel(side, cuts, lo_ref, group_ref, own_ref, other_ref, acc_ref, *refs):
    parts = len(cuts) - 1
    mine_refs, theirs_refs = refs[:parts], refs[parts : 2 * parts]
    keep_ref, send_refs = refs[2 * parts], refs[2 * parts + 1 :]
    hidden = mine_refs[0].shape[-1]
    first = group_ref[0] == 0
    for step in reversed(range(side)):
        x = row_chunk(own_ref, other_ref, lo_ref[0] ^ step, 1, side)
        mine = theirs = 0.0
        for part in range(parts):
            piece = x[:, cuts[part] : cuts[part + 1]]
            mine += jnp.dot(piece, mine_refs[part][...], preferred_element_type=jnp.float32)
            theirs += jnp.dot(piece, theirs_refs[part][...], preferred_element_type=jnp.float32)
        gate = acc_ref[step, :, :hidden] + jnp.where(first, mine, theirs)
        up = acc_ref[step, :, hidden:] + jnp.where(first, theirs, mine)
        target = send_refs[step - 1] if step else keep_ref
        target[:, :hidden] = gate.astype(target.dtype)
        target[:, hidden:] = up.astype(target.dtype)


def partial_first(lo, own, other, gate, up, side):
    chunk = 2 * own.shape[0] * own.shape[2] // side
    return pl.pallas_call(
        functools.partial(first_kernel, side),
        out_shape=jax.ShapeDtypeStruct((side, chunk, 2 * gate.shape[1]), jnp.float32),
        in_specs=[SMEM] + [WHOLE] * 4,
        out_specs=WHOLE,
        compiler_params=KERNEL,
    )(lo, own, other, gate, up)


def partial_second(lo, group, own, other, acc, mine, theirs, cuts, side):
    _, chunk, width = acc.shape
    keep = jax.ShapeDtypeStruct((chunk, width), jnp.float32)
    send = jax.ShapeDtypeStruct((chunk, width), jnp.bfloat16)
    return pl.pallas_call(
        functools.partial(second_kernel, side, cuts),
        out_shape=(keep,) + (send,) * (side - 1),
        in_specs=[SMEM] * 2 + [WHOLE] * (3 + 2 * len(mine)),
        out_specs=(WHOLE,) * side,
        compiler_params=KERNEL,
    )(lo, group, own, other, acc, *mine, *theirs)


def local(tokens, cotangent, expert_ids, gate_values, w_gate, w_up, feedback):
    token_count = tokens.shape[0]
    top_count = expert_ids.shape[1]
    nodes, side = lax.axis_size("node"), lax.axis_size("lo")
    capacity = max(2, token_count * top_count // nodes)
    width = tokens.shape[1] // (2 * side)
    half, lo, group = (lax.axis_index(a).astype(jnp.int32)[None] for a in ("hi", "lo", "groups"))
    gate_own, up_own = w_gate[0], w_up[0]

    cuts = tuple(range(0, width, 256)) + (width,)
    mine, theirs = [], []
    for start, end in zip(cuts, cuts[1:]):
        piece = jnp.where(group[0] == 0, gate_own[start:end], up_own[start:end])
        mine.append(swapped(piece, "hi"))
    theirs = [swapped(piece, "groups") for piece in mine]

    if top_count > 1:
        tokens = jnp.repeat(tokens, top_count, axis=0)
        cotangent = jnp.repeat(cotangent, top_count, axis=0)
    send_x, send_y = dispatch(
        half,
        expert_ids.reshape(1, -1),
        gate_values.reshape(1, -1),
        tokens,
        cotangent,
        nodes,
        side,
        capacity,
    )
    own_x = lax.all_to_all(send_x, ("node", "lo"), 0, 0, tiled=True)
    other_x = swapped(own_x, "rep")
    acc = partial_first(lo, own_x, other_x, gate_own, up_own, side)

    send_y, _ = lax.optimization_barrier((send_y, mine[-1]))
    own_y = lax.all_to_all(send_y, ("hi", "node", "lo"), 0, 0, tiled=True)
    other_y = swapped(own_y, "rep")

    keep, *sends = partial_second(lo, group, own_x, other_x, acc, mine, theirs, cuts, side)
    pre = keep
    for step, send in enumerate(sends, 1):
        pre = pre + swapped(send, "lo", step).astype(jnp.float32)
    pre_gate, pre_up = jnp.split(pre, 2, axis=1)
    hidden = (jax.nn.silu(pre_gate) * pre_up).astype(jnp.bfloat16)
    hidden = lax.all_gather(hidden, ("hi", "lo"), axis=0, tiled=True)
    y_rows = jnp.stack([own_y.reshape(2, -1, width), other_y.reshape(2, -1, width)], axis=1)
    grad = lax.dot_general(
        hidden,
        y_rows.reshape(-1, width),
        (((0,), (0,)), ((), ())),
        preferred_element_type=jnp.float32,
    )
    return (grad + feedback[0].astype(jnp.float32)).astype(jnp.bfloat16)[None]


def solution(mesh):
    names = ("groups", "node", "hi", "lo", "rep")
    groups, nodes, locals_, reps = (mesh.shape[a] for a in ("groups", "node", "local", "rep"))
    split = Mesh(mesh.devices.reshape(groups, nodes, 2, locals_ // 2, reps), names)
    rows = P(names, None)
    weights = P("node", ("hi", "lo"), "rep")
    return jax.shard_map(
        local,
        mesh=split,
        in_specs=(rows, rows, rows, rows, weights, weights, P("node", "rep", ("hi", "lo"))),
        out_specs=P(("groups", "node"), "rep", ("hi", "lo")),
        check_vma=False,
    )
```

```python
import functools

import jax
import jax.numpy as jnp
from jax import lax
from jax.experimental import pallas as pl
from jax.experimental.pallas import tpu as pltpu
from jax.sharding import Mesh
from jax.sharding import PartitionSpec as P

KERNEL = pltpu.CompilerParams(vmem_limit_bytes=40 << 20)
SMEM = pl.BlockSpec(memory_space=pltpu.SMEM)
WHOLE = pl.BlockSpec()
F32 = jnp.float32
BF16 = jnp.bfloat16


def cost(flops, *arrays):
    size = sum(a.size * a.dtype.itemsize for a in arrays)
    return pl.CostEstimate(flops=flops, bytes_accessed=size, transcendentals=0)


def swapped(value, axis, distance=1):
    pairs = [(s, s ^ distance) for s in range(lax.axis_size(axis))]
    return lax.ppermute(value, axis, pairs)


def dispatch_kernel(nodes, side, capacity, half_ref, ids_ref, gate_ref, x_ref, c_ref, sx_ref, sy_ref):
    pairs = ids_ref.shape[1]
    width = sx_ref.shape[-1]
    half = half_ref[0]
    ids = ids_ref[...]
    row = lax.broadcasted_iota(jnp.int32, (pairs, pairs), 0)
    col = lax.broadcasted_iota(jnp.int32, (pairs, pairs), 1)
    earlier = (row < col).astype(BF16)
    slots = lax.broadcasted_iota(jnp.int32, (capacity, pairs), 0)
    for node in range(nodes):
        named = ids == node
        rank = jnp.dot(
            jnp.broadcast_to(jnp.where(named, 1.0, 0.0), (8, pairs)).astype(BF16),
            earlier,
            preferred_element_type=F32,
        )[:1].astype(jnp.int32)
        pick = jnp.where((rank == slots) & named, 1.0, 0.0)
        gate = jnp.sum(pick * gate_ref[...], axis=1, keepdims=True)
        pick = pick.astype(BF16)
        for hi in range(2):
            for lo in range(side):
                block = hi * side + lo
                cols = slice(block * width, (block + 1) * width)
                x_rows = jnp.dot(pick, x_ref[:, cols], preferred_element_type=F32)
                c_rows = jnp.dot(pick, c_ref[:, cols], preferred_element_type=F32)
                sx_ref[node * side + lo, half ^ hi] = x_rows.astype(BF16)
                sy_ref[(hi * nodes + node) * side + lo] = (gate * c_rows).astype(BF16)


def dispatch(half, ids, gates, tokens, cotangent, nodes, side, capacity):
    width = tokens.shape[1] // (2 * side)
    return pl.pallas_call(
        functools.partial(dispatch_kernel, nodes, side, capacity),
        out_shape=(
            jax.ShapeDtypeStruct((nodes * side, 2, capacity, width), BF16),
            jax.ShapeDtypeStruct((2 * nodes * side, capacity, width), BF16),
        ),
        in_specs=[SMEM] + [WHOLE] * 4,
        out_specs=(WHOLE, WHOLE),
        compiler_params=KERNEL,
        cost_estimate=cost(4 * nodes * capacity * tokens.size, tokens, cotangent, tokens, cotangent),
    )(half, ids, gates, tokens, cotangent)


def row_chunk(own_ref, other_ref, index, quarter, side):
    per_core = side // 2
    count = own_ref.shape[0] // per_core
    place = index % per_core
    own = own_ref[pl.ds(place * count, count), quarter]
    other = other_ref[pl.ds(place * count, count), quarter]
    rows = jnp.where(index < per_core, own, other)
    return rows.reshape(-1, rows.shape[-1])


def first_kernel(side, lo_ref, group_ref, own_ref, other_ref, gate_ref, up_ref, mine_ref, theirs_ref):
    first = group_ref[0] == 0
    for step in range(side):
        x = row_chunk(own_ref, other_ref, lo_ref[0] ^ step, 0, side)
        gate = jnp.dot(x, gate_ref[...], preferred_element_type=F32)
        up = jnp.dot(x, up_ref[...], preferred_element_type=F32)
        mine_ref[step] = jnp.where(first, gate, up)
        theirs_ref[step] = jnp.where(first, up, gate)


def second_kernel(side, steps, lo_ref, own_ref, other_ref, acc_ref, weight_ref, *out_refs):
    for step, out_ref in zip(steps, out_refs):
        x = row_chunk(own_ref, other_ref, lo_ref[0] ^ step, 1, side)
        pre = acc_ref[step] + jnp.dot(x, weight_ref[...], preferred_element_type=F32)
        out_ref[...] = pre.astype(out_ref.dtype)


def partial_first(lo, group, own, other, gate, up, side):
    chunk = 2 * own.shape[0] * own.shape[2] // side
    acc = jax.ShapeDtypeStruct((side, chunk, gate.shape[1]), F32)
    return pl.pallas_call(
        functools.partial(first_kernel, side),
        out_shape=(acc, acc),
        in_specs=[SMEM] * 2 + [WHOLE] * 4,
        out_specs=(WHOLE, WHOLE),
        compiler_params=KERNEL,
        cost_estimate=cost(4 * side * chunk * gate.size, own, other, gate, up),
    )(lo, group, own, other, gate, up)


def partial_second(lo, own, other, acc, weight, side, steps, dtype):
    _, chunk, width = acc.shape
    out = jax.ShapeDtypeStruct((chunk, width), dtype)
    return pl.pallas_call(
        functools.partial(second_kernel, side, steps),
        out_shape=(out,) * len(steps),
        in_specs=[SMEM] + [WHOLE] * 4,
        out_specs=(WHOLE,) * len(steps),
        compiler_params=KERNEL,
        cost_estimate=cost(2 * len(steps) * chunk * weight.size, own, other, weight),
    )(lo, own, other, acc, weight)


def pair_sum(lo, own, other, acc, weight, side):
    sends = partial_second(lo, own, other, acc, weight, side, range(1, side), BF16)
    came = [swapped(send, "lo", step) for step, send in enumerate(sends, 1)]
    total = partial_second(lo, own, other, acc, weight, side, (0,), F32)[0]
    for part in came:
        total = total + part.astype(F32)
    return total


def block_product(hidden_ref, y_own_ref, y_other_ref, hi, lo):
    rows = jnp.where(lo == 0, y_own_ref[hi], y_other_ref[hi])
    return lax.dot_general(
        hidden_ref[...], rows, (((0,), (0,)), ((), ())), preferred_element_type=F32
    )


def near_kernel(hi_ref, lo_ref, own_ref, beside_ref, y_own_ref, y_other_ref, feedback_ref, out_ref):
    hi, lo = hi_ref[0], lo_ref[0]
    total = block_product(own_ref, y_own_ref, y_other_ref, hi, lo)
    total += block_product(beside_ref, y_own_ref, y_other_ref, hi, 1 - lo)
    out_ref[...] = total + feedback_ref[...].astype(F32)


def far_kernel(hi_ref, lo_ref, across_ref, corner_ref, y_own_ref, y_other_ref, near_ref, out_ref):
    hi, lo = hi_ref[0], lo_ref[0]
    total = block_product(across_ref, y_own_ref, y_other_ref, 1 - hi, lo)
    total += block_product(corner_ref, y_own_ref, y_other_ref, 1 - hi, 1 - lo)
    out_ref[...] = (near_ref[...] + total).astype(BF16)


def two_blocks(kernel, hi, lo, first, second, y_own, y_other, base, dtype):
    shape = (first.shape[1], y_own.shape[2])
    return pl.pallas_call(
        kernel,
        out_shape=jax.ShapeDtypeStruct(shape, dtype),
        in_specs=[SMEM] * 2 + [WHOLE] * 5,
        out_specs=WHOLE,
        compiler_params=KERNEL,
        cost_estimate=cost(4 * first.size * y_own.shape[2], first, second, y_own, y_other, base),
    )(hi, lo, first, second, y_own, y_other, base)


def product(hi, lo, hidden, own_y, other_y, feedback, side):
    width = own_y.shape[-1]
    own_y, other_y = own_y.reshape(2, -1, width), other_y.reshape(2, -1, width)
    if side == 2:
        across = swapped(hidden, "hi")
        beside = swapped(hidden, "lo")
        corner = swapped(across, "lo")
        near = two_blocks(near_kernel, hi, lo, hidden, beside, own_y, other_y, feedback, F32)
        return two_blocks(far_kernel, hi, lo, across, corner, own_y, other_y, near, BF16)
    hidden = lax.all_gather(hidden, ("hi", "lo"), axis=0, tiled=True)
    y_rows = jnp.stack([own_y, other_y], axis=1).reshape(-1, width)
    grad = lax.dot_general(hidden, y_rows, (((0,), (0,)), ((), ())), preferred_element_type=F32)
    return (grad + feedback.astype(F32)).astype(BF16)


def local(tokens, cotangent, expert_ids, gate_values, w_gate, w_up, feedback):
    token_count = tokens.shape[0]
    top_count = expert_ids.shape[1]
    nodes, side = lax.axis_size("node"), lax.axis_size("lo")
    capacity = max(2, token_count * top_count // nodes)
    hi, lo, group = (lax.axis_index(a).astype(jnp.int32)[None] for a in ("hi", "lo", "groups"))
    gate_own, up_own = w_gate[0], w_up[0]
    first = group[0] == 0

    piece = jnp.where(first, gate_own, up_own)
    tokens, piece = lax.optimization_barrier((tokens, piece))
    mine = swapped(piece, "hi")
    theirs = swapped(mine, "groups")

    if top_count > 1:
        tokens = jnp.repeat(tokens, top_count, axis=0)
        cotangent = jnp.repeat(cotangent, top_count, axis=0)
    send_x, send_y = dispatch(
        hi,
        expert_ids.reshape(1, -1),
        gate_values.reshape(1, -1),
        tokens,
        cotangent,
        nodes,
        side,
        capacity,
    )
    own_x = lax.all_to_all(send_x, ("node", "lo"), 0, 0, tiled=True)
    other_x = swapped(own_x, "rep")
    acc_mine, acc_theirs = partial_first(lo, group, own_x, other_x, gate_own, up_own, side)

    send_y, _ = lax.optimization_barrier((send_y, mine))
    own_y = lax.all_to_all(send_y, ("hi", "node", "lo"), 0, 0, tiled=True)
    other_y = swapped(own_y, "rep")

    pre_mine = pair_sum(lo, own_x, other_x, acc_mine, mine, side)
    pre_theirs = pair_sum(lo, own_x, other_x, acc_theirs, theirs, side)
    pre_gate = jnp.where(first, pre_mine, pre_theirs)
    pre_up = jnp.where(first, pre_theirs, pre_mine)
    hidden = (jax.nn.silu(pre_gate) * pre_up).astype(BF16)
    return product(hi, lo, hidden, own_y, other_y, feedback[0], side)[None]


def solution(mesh):
    names = ("groups", "node", "hi", "lo", "rep")
    groups, nodes, locals_, reps = (mesh.shape[a] for a in ("groups", "node", "local", "rep"))
    split = Mesh(mesh.devices.reshape(groups, nodes, 2, locals_ // 2, reps), names)
    rows = P(names, None)
    weights = P("node", ("hi", "lo"), "rep")
    return jax.shard_map(
        local,
        mesh=split,
        in_specs=(rows, rows, rows, rows, weights, weights, P("node", "rep", ("hi", "lo"))),
        out_specs=P(("groups", "node"), "rep", ("hi", "lo")),
        check_vma=False,
    )
```

```python
import functools

import jax
import jax.numpy as jnp
from jax import lax
from jax.experimental import pallas as pl
from jax.experimental.pallas import tpu as pltpu
from jax.sharding import Mesh
from jax.sharding import PartitionSpec as P


CUT = 384
KERNEL = pltpu.CompilerParams(vmem_limit_bytes=40 << 20)
SMEM = pl.BlockSpec(memory_space=pltpu.SMEM)
WHOLE = pl.BlockSpec()
F32 = jnp.float32
BF16 = jnp.bfloat16


def call(kernel, flops, outs, scalars, arrays):
    size = sum(a.size * a.dtype.itemsize for a in (*arrays, *outs))
    return pl.pallas_call(
        kernel,
        out_shape=outs,
        in_specs=[SMEM] * len(scalars) + [WHOLE] * len(arrays),
        out_specs=(WHOLE,) * len(outs),
        compiler_params=KERNEL,
        cost_estimate=pl.CostEstimate(flops=flops, bytes_accessed=size, transcendentals=0),
    )(*scalars, *arrays)


def shape(dims, dtype):
    return jax.ShapeDtypeStruct(dims, dtype)


def swapped(value, axis, distance=1):
    pairs = [(s, s ^ distance) for s in range(lax.axis_size(axis))]
    return lax.ppermute(value, axis, pairs)


def dispatch_kernel(nodes, side, capacity, node_ref, hi_ref, lo_ref, ids_ref, gate_ref, x_ref, c_ref, *out_refs):
    pairs = ids_ref.shape[1]
    sx_refs, sy_refs = out_refs[:nodes], out_refs[nodes:]
    width = sx_refs[0].shape[-1]
    ids = ids_ref[...]
    row = lax.broadcasted_iota(jnp.int32, (pairs, pairs), 0)
    col = lax.broadcasted_iota(jnp.int32, (pairs, pairs), 1)
    earlier = (row < col).astype(BF16)
    slots = lax.broadcasted_iota(jnp.int32, (capacity, pairs), 0)
    for step in range(nodes):
        named = ids == (node_ref[0] ^ step)
        rank = jnp.dot(
            jnp.broadcast_to(jnp.where(named, 1.0, 0.0), (8, pairs)).astype(BF16),
            earlier,
            preferred_element_type=F32,
        )[:1].astype(jnp.int32)
        pick = jnp.where((rank == slots) & named, 1.0, 0.0)
        gate = jnp.sum(pick * gate_ref[...], axis=1, keepdims=True)
        pick = pick.astype(BF16)
        for hi in range(2):
            for lo in range(side):
                block = hi * side + lo
                cols = slice(block * width, (block + 1) * width)
                x_rows = jnp.dot(pick, x_ref[:, cols], preferred_element_type=F32)
                c_rows = jnp.dot(pick, c_ref[:, cols], preferred_element_type=F32)
                sx_refs[step][lo_ref[0] ^ lo, hi_ref[0] ^ hi] = x_rows.astype(BF16)
                sy_refs[step][hi_ref[0] ^ hi, lo_ref[0] ^ lo] = (gate * c_rows).astype(BF16)


def dispatch(node, hi, lo, ids, gates, tokens, cotangent, nodes, side, capacity):
    width = tokens.shape[1] // (2 * side)
    x = shape((side, 2, capacity, width), BF16)
    y = shape((2, side, capacity, width), BF16)
    outs = call(
        functools.partial(dispatch_kernel, nodes, side, capacity),
        4 * nodes * capacity * tokens.size,
        (x,) * nodes + (y,) * nodes,
        (node, hi, lo),
        (ids, gates, tokens, cotangent),
    )
    return outs[:nodes], outs[nodes:]


def owned_rows(own_ref, other_ref, lo, step, pick, nodes, side):
    owner = lo ^ step
    per_core = side // 2
    count = nodes // per_core
    place = (owner % per_core) * count
    rows = []
    for source in range(side):
        own = pick(own_ref, step ^ source, pl.ds(place, count))
        other = pick(other_ref, step ^ source, pl.ds(place, count))
        chosen = jnp.where(owner < per_core, own, other)
        rows.append(chosen.reshape(-1, chosen.shape[-1]))
    return jnp.concatenate(rows, axis=0)


def first_kernel(nodes, side, lo_ref, group_ref, own_ref, other_ref, gate_ref, up_ref, mine_ref, theirs_ref):
    first = group_ref[0] == 0
    half = gate_ref.shape[1] // 2
    for step in range(side):
        pick = lambda ref, source, part: ref[source, part, 0]
        x = owned_rows(own_ref, other_ref, lo_ref[0], step, pick, nodes, side)
        for place, weight_ref in enumerate((gate_ref, up_ref)):
            pre = jnp.dot(x, weight_ref[...], preferred_element_type=F32)
            cols = slice(place * half, (place + 1) * half)
            mine_ref[step, :, cols] = jnp.where(first, pre[:, :half], pre[:, half:])
            theirs_ref[step, :, cols] = jnp.where(first, pre[:, half:], pre[:, :half])


def second_kernel(nodes, side, steps, cuts, lo_ref, own_ref, other_ref, acc_ref, *refs):
    parts = len(cuts) - 1
    weight_refs, out_refs = refs[:parts], refs[parts:]
    for step, out_ref in zip(steps, out_refs):
        pick = lambda ref, source, part: ref[source, part, 1]
        x = owned_rows(own_ref, other_ref, lo_ref[0], step, pick, nodes, side)
        pre = acc_ref[step]
        for start, end, weight_ref in zip(cuts, cuts[1:], weight_refs):
            pre += jnp.dot(x[:, start:end], weight_ref[...], preferred_element_type=F32)
        out_ref[...] = pre.astype(out_ref.dtype)


def partial_first(lo, group, own, other, gate, up, nodes, side):
    chunk = 2 * nodes * own.shape[3]
    acc = shape((side, chunk, gate.shape[1]), F32)
    return call(
        functools.partial(first_kernel, nodes, side),
        4 * side * chunk * gate.size,
        (acc, acc),
        (lo, group),
        (own, other, gate, up),
    )


def partial_second(lo, own, other, acc, weights, cuts, nodes, side, steps, dtype):
    out = shape(acc.shape[1:], dtype)
    return call(
        functools.partial(second_kernel, nodes, side, steps, cuts),
        2 * len(steps) * acc.shape[1] * cuts[-1] * acc.shape[2],
        (out,) * len(steps),
        (lo,),
        (own, other, acc, *weights),
    )


def block_product(nodes, side, hidden_ref, own_ref, other_ref, lo, place):
    hi_step, lo_step = place
    pick = lambda ref, source, part: ref[hi_step, source, part]
    rows = owned_rows(own_ref, other_ref, lo, lo_step, pick, nodes, side)
    return lax.dot_general(
        hidden_ref[...], rows, (((0,), (0,)), ((), ())), preferred_element_type=F32
    )


def near_kernel(nodes, side, lo_ref, group_ref, *refs):
    blocks, (own_ref, other_ref, feedback_ref, done_ref, base_ref) = refs[:-5], refs[-5:]
    half = done_ref.shape[0]
    places = [(h, l) for h in range(2) for l in range(side)]
    sums = []
    for start, count, which in ((0, 2 * side, group_ref[0]), (2 * side, side, 1 - group_ref[0])):
        total = feedback_ref[pl.ds(pl.multiple_of(which * half, half), half), :].astype(F32)
        for block_ref, place in zip(blocks[start : start + count], places):
            total += block_product(nodes, side, block_ref, own_ref, other_ref, lo_ref[0], place)
        sums.append(total)
    done_ref[...] = sums[0].astype(BF16)
    base_ref[...] = sums[1]


def far_kernel(nodes, side, lo_ref, group_ref, *refs):
    blocks, (own_ref, other_ref, done_ref, base_ref, out_ref) = refs[:-5], refs[-5:]
    half = done_ref.shape[0]
    total = base_ref[...]
    for step, block_ref in enumerate(blocks):
        total += block_product(nodes, side, block_ref, own_ref, other_ref, lo_ref[0], (1, step))
    mine, theirs = group_ref[0], 1 - group_ref[0]
    out_ref[pl.ds(pl.multiple_of(mine * half, half), half), :] = done_ref[...]
    out_ref[pl.ds(pl.multiple_of(theirs * half, half), half), :] = total.astype(BF16)


def product(lo, group, first, second, own, other, feedback, nodes, side):
    half, width = first[0].shape[1], own.shape[-1]
    flops = 2 * first[0].size * width
    done, base = call(
        functools.partial(near_kernel, nodes, side),
        3 * side * flops,
        (shape((half, width), BF16), shape((half, width), F32)),
        (lo, group),
        (*first, *second[:side], own, other, feedback),
    )
    return call(
        functools.partial(far_kernel, nodes, side),
        side * flops,
        (shape((2 * half, width), BF16),),
        (lo, group),
        (*second[side:], own, other, done, base),
    )[0]


def local(tokens, cotangent, expert_ids, gate_values, w_gate, w_up, feedback):
    token_count = tokens.shape[0]
    top_count = expert_ids.shape[1]
    nodes, side = lax.axis_size("node"), lax.axis_size("lo")
    capacity = max(2, token_count * top_count // nodes)
    node, hi, lo, group = (
        lax.axis_index(a).astype(jnp.int32)[None] for a in ("node", "hi", "lo", "groups")
    )
    gate_own, up_own = w_gate[0], w_up[0]
    half = gate_own.shape[1] // 2
    width = gate_own.shape[0]
    cuts = (0, CUT, width) if width > CUT else (0, width)
    pieces = []
    for rows in (slice(*pair) for pair in zip(cuts, cuts[1:])):
        left = jnp.concatenate([gate_own[rows, :half], up_own[rows, :half]], axis=1)
        right = jnp.concatenate([gate_own[rows, half:], up_own[rows, half:]], axis=1)
        pieces.append(jnp.where(group[0] == 0, left, right))
    tokens, pieces = lax.optimization_barrier((tokens, pieces))
    mine = [swapped(piece, "hi") for piece in pieces]
    theirs = [swapped(piece, "groups") for piece in mine[:-1]]

    if top_count > 1:
        tokens = jnp.repeat(tokens, top_count, axis=0)
        cotangent = jnp.repeat(cotangent, top_count, axis=0)
    send_x, send_y = dispatch(
        node,
        hi,
        lo,
        expert_ids.reshape(1, -1),
        gate_values.reshape(1, -1),
        tokens,
        cotangent,
        nodes,
        side,
        capacity,
    )

    x = [send_x[0]] + [swapped(send_x[d], "node", d) for d in range(1, nodes)]
    x = [jnp.stack([part[d] for part in x]) for d in range(side)]
    x, mine[0] = lax.optimization_barrier((x, mine[0]))
    own_x = jnp.stack([x[0]] + [swapped(x[d], "lo", d) for d in range(1, side)])
    own_x, theirs = lax.optimization_barrier((own_x, theirs))
    other_x = swapped(own_x, "rep")
    acc_mine, acc_theirs = partial_first(lo, group, own_x, other_x, gate_own, up_own, nodes, side)
    mine[-1], acc_mine, acc_theirs = lax.optimization_barrier((mine[-1], acc_mine, acc_theirs))
    theirs.append(swapped(mine[-1], "groups"))

    y = [send_y[0]] + [swapped(send_y[d], "node", d) for d in range(1, nodes)]
    y = [[jnp.stack([part[h, l] for part in y]) for l in range(side)] for h in range(2)]
    y, mine[-1] = lax.optimization_barrier((y, mine[-1]))
    for h in range(2):
        for l in range(side):
            if (h, l) != (0, 0):
                pairs = [(s, s ^ (h * side + l)) for s in range(2 * side)]
                y[h][l] = lax.ppermute(y[h][l], ("hi", "lo"), pairs)
    own_y = jnp.stack([jnp.stack(row) for row in y])
    other_y = swapped(own_y, "rep")

    def spread_hidden(acc, weights):
        args = (lo, own_x, other_x, acc, weights, cuts, nodes, side)
        sends = partial_second(*args, range(1, side), BF16)
        came = [swapped(send, "lo", d) for d, send in enumerate(sends, 1)]
        pre = partial_second(*args, (0,), F32)[0]
        for part in came:
            pre = pre + part.astype(F32)
        hidden = (jax.nn.silu(pre[:, :half]) * pre[:, half:]).astype(BF16)
        across = swapped(hidden, "hi")
        beside = [swapped(hidden, "lo", d) for d in range(1, side)]
        corners = [swapped(across, "lo", d) for d in range(1, side)]
        return [hidden, *beside, across, *corners]

    first = spread_hidden(acc_mine, mine)
    first[0], theirs = lax.optimization_barrier((first[0], theirs))
    second = spread_hidden(acc_theirs, theirs)
    return product(lo, group, first, second, own_y, other_y, feedback[0], nodes, side)[None]


def solution(mesh):
    names = ("groups", "node", "hi", "lo", "rep")
    groups, nodes, locals_, reps = (mesh.shape[a] for a in ("groups", "node", "local", "rep"))
    split = Mesh(mesh.devices.reshape(groups, nodes, 2, locals_ // 2, reps), names)
    rows = P(names, None)
    weights = P("node", ("hi", "lo"), "rep")
    return jax.shard_map(
        local,
        mesh=split,
        in_specs=(rows, rows, rows, rows, weights, weights, P("node", "rep", ("hi", "lo"))),
        out_specs=P(("groups", "node"), "rep", ("hi", "lo")),
        check_vma=False,
    )
```

```python
import functools

import jax
import jax.numpy as jnp
from jax import lax
from jax.experimental import pallas as pl
from jax.experimental.pallas import tpu as pltpu
from jax.sharding import Mesh
from jax.sharding import PartitionSpec as P


CUT = 100000
KERNEL = pltpu.CompilerParams(vmem_limit_bytes=40 << 20)
SMEM = pl.BlockSpec(memory_space=pltpu.SMEM)
WHOLE = pl.BlockSpec()
F32 = jnp.float32
BF16 = jnp.bfloat16


def call(kernel, flops, outs, scalars, arrays):
    size = sum(a.size * a.dtype.itemsize for a in (*arrays, *outs))
    return pl.pallas_call(
        kernel,
        out_shape=outs,
        in_specs=[SMEM] * len(scalars) + [WHOLE] * len(arrays),
        out_specs=(WHOLE,) * len(outs),
        compiler_params=KERNEL,
        cost_estimate=pl.CostEstimate(flops=flops, bytes_accessed=size, transcendentals=0),
    )(*scalars, *arrays)


def shape(dims, dtype):
    return jax.ShapeDtypeStruct(dims, dtype)


def swapped(value, axis, distance=1):
    pairs = [(s, s ^ distance) for s in range(lax.axis_size(axis))]
    return lax.ppermute(value, axis, pairs)


def dispatch_kernel(nodes, side, capacity, node_ref, hi_ref, lo_ref, ids_ref, gate_ref, x_ref, c_ref, *out_refs):
    pairs = ids_ref.shape[1]
    sx_refs, sy_refs = out_refs[:nodes], out_refs[nodes:]
    width = sx_refs[0].shape[-1]
    ids = ids_ref[...]
    row = lax.broadcasted_iota(jnp.int32, (pairs, pairs), 0)
    col = lax.broadcasted_iota(jnp.int32, (pairs, pairs), 1)
    earlier = (row < col).astype(BF16)
    slots = lax.broadcasted_iota(jnp.int32, (capacity, pairs), 0)
    for step in range(nodes):
        named = ids == (node_ref[0] ^ step)
        rank = jnp.dot(
            jnp.broadcast_to(jnp.where(named, 1.0, 0.0), (8, pairs)).astype(BF16),
            earlier,
            preferred_element_type=F32,
        )[:1].astype(jnp.int32)
        pick = jnp.where((rank == slots) & named, 1.0, 0.0)
        gate = jnp.sum(pick * gate_ref[...], axis=1, keepdims=True)
        pick = pick.astype(BF16)
        for hi in range(2):
            for lo in range(side):
                block = hi * side + lo
                cols = slice(block * width, (block + 1) * width)
                x_rows = jnp.dot(pick, x_ref[:, cols], preferred_element_type=F32)
                c_rows = jnp.dot(pick, c_ref[:, cols], preferred_element_type=F32)
                sx_refs[step][lo_ref[0] ^ lo, hi_ref[0] ^ hi] = x_rows.astype(BF16)
                sy_refs[step][hi_ref[0] ^ hi, lo_ref[0] ^ lo] = (gate * c_rows).astype(BF16)


def dispatch(node, hi, lo, ids, gates, tokens, cotangent, nodes, side, capacity):
    width = tokens.shape[1] // (2 * side)
    x = shape((side, 2, capacity, width), BF16)
    y = shape((2, side, capacity, width), BF16)
    outs = call(
        functools.partial(dispatch_kernel, nodes, side, capacity),
        4 * nodes * capacity * tokens.size,
        (x,) * nodes + (y,) * nodes,
        (node, hi, lo),
        (ids, gates, tokens, cotangent),
    )
    return outs[:nodes], outs[nodes:]


def owned_rows(own_ref, other_ref, lo, step, pick, nodes, side):
    owner = lo ^ step
    per_core = side // 2
    count = nodes // per_core
    place = (owner % per_core) * count
    rows = []
    for source in range(side):
        own = pick(own_ref, step ^ source, pl.ds(place, count))
        other = pick(other_ref, step ^ source, pl.ds(place, count))
        chosen = jnp.where(owner < per_core, own, other)
        rows.append(chosen.reshape(-1, chosen.shape[-1]))
    return jnp.concatenate(rows, axis=0)


def first_kernel(nodes, side, lo_ref, group_ref, own_ref, other_ref, gate_ref, up_ref, mine_ref, theirs_ref):
    first = group_ref[0] == 0
    half = gate_ref.shape[1] // 2
    for step in range(side):
        pick = lambda ref, source, part: ref[source, part, 0]
        x = owned_rows(own_ref, other_ref, lo_ref[0], step, pick, nodes, side)
        for place, weight_ref in enumerate((gate_ref, up_ref)):
            pre = jnp.dot(x, weight_ref[...], preferred_element_type=F32)
            cols = slice(place * half, (place + 1) * half)
            mine_ref[step, :, cols] = jnp.where(first, pre[:, :half], pre[:, half:])
            theirs_ref[step, :, cols] = jnp.where(first, pre[:, half:], pre[:, :half])


def second_kernel(nodes, side, steps, cuts, lo_ref, own_ref, other_ref, acc_ref, *refs):
    parts = len(cuts) - 1
    weight_refs, out_refs = refs[:parts], refs[parts:]
    for step, out_ref in zip(steps, out_refs):
        pick = lambda ref, source, part: ref[source, part, 1]
        x = owned_rows(own_ref, other_ref, lo_ref[0], step, pick, nodes, side)
        pre = acc_ref[step]
        for start, end, weight_ref in zip(cuts, cuts[1:], weight_refs):
            pre += jnp.dot(x[:, start:end], weight_ref[...], preferred_element_type=F32)
        out_ref[...] = pre.astype(out_ref.dtype)


def partial_first(lo, group, own, other, gate, up, nodes, side):
    chunk = 2 * nodes * own.shape[3]
    acc = shape((side, chunk, gate.shape[1]), F32)
    return call(
        functools.partial(first_kernel, nodes, side),
        4 * side * chunk * gate.size,
        (acc, acc),
        (lo, group),
        (own, other, gate, up),
    )


def partial_second(lo, own, other, acc, weights, cuts, nodes, side, steps, dtype):
    out = shape(acc.shape[1:], dtype)
    return call(
        functools.partial(second_kernel, nodes, side, steps, cuts),
        2 * len(steps) * acc.shape[1] * cuts[-1] * acc.shape[2],
        (out,) * len(steps),
        (lo,),
        (own, other, acc, *weights),
    )


def block_product(nodes, side, hidden_ref, own_ref, other_ref, lo, place):
    hi_step, lo_step = place
    pick = lambda ref, source, part: ref[hi_step, source, part]
    rows = owned_rows(own_ref, other_ref, lo, lo_step, pick, nodes, side)
    return lax.dot_general(
        hidden_ref[...], rows, (((0,), (0,)), ((), ())), preferred_element_type=F32
    )


def near_kernel(nodes, side, lo_ref, group_ref, *refs):
    blocks, (own_ref, other_ref, feedback_ref, done_ref, base_ref) = refs[:-5], refs[-5:]
    half = done_ref.shape[0]
    places = [(h, l) for h in range(2) for l in range(side)]
    sums = []
    for start, count, which in ((0, 2 * side, group_ref[0]), (2 * side, side, 1 - group_ref[0])):
        total = feedback_ref[pl.ds(pl.multiple_of(which * half, half), half), :].astype(F32)
        for block_ref, place in zip(blocks[start : start + count], places):
            total += block_product(nodes, side, block_ref, own_ref, other_ref, lo_ref[0], place)
        sums.append(total)
    done_ref[...] = sums[0].astype(BF16)
    base_ref[...] = sums[1]


def far_kernel(nodes, side, lo_ref, group_ref, *refs):
    blocks, (own_ref, other_ref, done_ref, base_ref, out_ref) = refs[:-5], refs[-5:]
    half = done_ref.shape[0]
    total = base_ref[...]
    for step, block_ref in enumerate(blocks):
        total += block_product(nodes, side, block_ref, own_ref, other_ref, lo_ref[0], (1, step))
    mine, theirs = group_ref[0], 1 - group_ref[0]
    out_ref[pl.ds(pl.multiple_of(mine * half, half), half), :] = done_ref[...]
    out_ref[pl.ds(pl.multiple_of(theirs * half, half), half), :] = total.astype(BF16)


def product(lo, group, first, second, own, other, feedback, nodes, side):
    half, width = first[0].shape[1], own.shape[-1]
    flops = 2 * first[0].size * width
    done, base = call(
        functools.partial(near_kernel, nodes, side),
        3 * side * flops,
        (shape((half, width), BF16), shape((half, width), F32)),
        (lo, group),
        (*first, *second[:side], own, other, feedback),
    )
    return call(
        functools.partial(far_kernel, nodes, side),
        side * flops,
        (shape((2 * half, width), BF16),),
        (lo, group),
        (*second[side:], own, other, done, base),
    )[0]


def local(tokens, cotangent, expert_ids, gate_values, w_gate, w_up, feedback):
    token_count = tokens.shape[0]
    top_count = expert_ids.shape[1]
    nodes, side = lax.axis_size("node"), lax.axis_size("lo")
    capacity = max(2, token_count * top_count // nodes)
    node, hi, lo, group = (
        lax.axis_index(a).astype(jnp.int32)[None] for a in ("node", "hi", "lo", "groups")
    )
    gate_own, up_own = w_gate[0], w_up[0]
    half = gate_own.shape[1] // 2
    width = gate_own.shape[0]
    cuts = (0, CUT, width) if width > CUT else (0, width)
    pieces = []
    for rows in (slice(*pair) for pair in zip(cuts, cuts[1:])):
        left = jnp.concatenate([gate_own[rows, :half], up_own[rows, :half]], axis=1)
        right = jnp.concatenate([gate_own[rows, half:], up_own[rows, half:]], axis=1)
        pieces.append(jnp.where(group[0] == 0, left, right))
    tokens, pieces = lax.optimization_barrier((tokens, pieces))
    mine = [swapped(piece, "hi") for piece in pieces]
    theirs = [swapped(piece, "groups") for piece in mine[:-1]]

    if top_count > 1:
        tokens = jnp.repeat(tokens, top_count, axis=0)
        cotangent = jnp.repeat(cotangent, top_count, axis=0)
    send_x, send_y = dispatch(
        node,
        hi,
        lo,
        expert_ids.reshape(1, -1),
        gate_values.reshape(1, -1),
        tokens,
        cotangent,
        nodes,
        side,
        capacity,
    )

    def spread_hidden(pre, came):
        for part in came:
            pre = pre + part.astype(F32)
        hidden = (jax.nn.silu(pre[:, :half]) * pre[:, half:]).astype(BF16)
        across = swapped(hidden, "hi")
        beside = [swapped(hidden, "lo", d) for d in range(1, side)]
        corners = [swapped(across, "lo", d) for d in range(1, side)]
        return [hidden, *beside, across, *corners]

    x = [send_x[0]] + [swapped(send_x[d], "node", d) for d in range(1, nodes)]
    x = [jnp.stack([part[d] for part in x]) for d in range(side)]
    y = [send_y[0]] + [swapped(send_y[d], "node", d) for d in range(1, nodes)]
    y = [[jnp.stack([part[h, l] for part in y]) for l in range(side)] for h in range(2)]
    own_x = jnp.stack([x[0]] + [swapped(x[d], "lo", d) for d in range(1, side)])
    own_x, mine[-1] = lax.optimization_barrier((own_x, mine[-1]))
    other_x = swapped(own_x, "rep")
    acc_mine, acc_theirs = partial_first(lo, group, own_x, other_x, gate_own, up_own, nodes, side)
    theirs.append(swapped(mine[-1], "groups"))
    margs = (lo, own_x, other_x, acc_mine, mine, cuts, nodes, side)
    sends_m = partial_second(*margs, range(1, side), BF16)
    y, mine[-1] = lax.optimization_barrier((y, mine[-1]))
    for h in range(2):
        for l in range(side):
            if (h, l) != (0, 0):
                pairs = [(s, s ^ (h * side + l)) for s in range(2 * side)]
                y[h][l] = lax.ppermute(y[h][l], ("hi", "lo"), pairs)
    came_m = [swapped(send, "lo", d) for d, send in enumerate(sends_m, 1)]
    keep_m = partial_second(*margs, (0,), F32)[0]
    first = spread_hidden(keep_m, came_m)
    own_y = jnp.stack([jnp.stack(row) for row in y])
    other_y = swapped(own_y, "rep")
    first[0], theirs = lax.optimization_barrier((first[0], theirs))
    targs = (lo, own_x, other_x, acc_theirs, theirs, cuts, nodes, side)
    sends_t = partial_second(*targs, range(1, side), BF16)
    came_t = [swapped(send, "lo", d) for d, send in enumerate(sends_t, 1)]
    keep_t = partial_second(*targs, (0,), F32)[0]
    second = spread_hidden(keep_t, came_t)
    return product(lo, group, first, second, own_y, other_y, feedback[0], nodes, side)[None]


def solution(mesh):
    names = ("groups", "node", "hi", "lo", "rep")
    groups, nodes, locals_, reps = (mesh.shape[a] for a in ("groups", "node", "local", "rep"))
    split = Mesh(mesh.devices.reshape(groups, nodes, 2, locals_ // 2, reps), names)
    rows = P(names, None)
    weights = P("node", ("hi", "lo"), "rep")
    return jax.shard_map(
        local,
        mesh=split,
        in_specs=(rows, rows, rows, rows, weights, weights, P("node", "rep", ("hi", "lo"))),
        out_specs=P(("groups", "node"), "rep", ("hi", "lo")),
        check_vma=False,
    )
```

```python
import functools

import jax
import jax.numpy as jnp
from jax import lax
from jax.experimental import pallas as pl
from jax.experimental.pallas import tpu as pltpu
from jax.sharding import Mesh
from jax.sharding import PartitionSpec as P


KERNEL = pltpu.CompilerParams(vmem_limit_bytes=40 << 20)
SMEM = pl.BlockSpec(memory_space=pltpu.SMEM)
WHOLE = pl.BlockSpec()
F32 = jnp.float32
BF16 = jnp.bfloat16


def call(kernel, flops, outs, scalars, arrays):
    size = sum(a.size * a.dtype.itemsize for a in (*arrays, *outs))
    return pl.pallas_call(
        kernel,
        out_shape=outs,
        in_specs=[SMEM] * len(scalars) + [WHOLE] * len(arrays),
        out_specs=(WHOLE,) * len(outs),
        compiler_params=KERNEL,
        cost_estimate=pl.CostEstimate(flops=flops, bytes_accessed=size, transcendentals=0),
    )(*scalars, *arrays)


def shape(dims, dtype):
    return jax.ShapeDtypeStruct(dims, dtype)


def swapped(value, axis, distance=1):
    pairs = [(s, s ^ distance) for s in range(lax.axis_size(axis))]
    return lax.ppermute(value, axis, pairs)


def pick_kernel(group_ref, gate_hbm, up_hbm, out_hbm, held, in_sems, out_sems):
    half = gate_hbm.shape[1] // 2
    count = gate_hbm.shape[0] // 2
    cols = pl.ds(pl.multiple_of(group_ref[0] * half, half), half)
    loads, stores = [], []
    for part in range(2):
        rows = pl.ds(part * count, count)
        for place, source in enumerate((gate_hbm, up_hbm)):
            target = held.at[rows, pl.ds(place * half, half)]
            loads.append(
                pltpu.make_async_copy(source.at[rows, cols], target, in_sems.at[part, place])
            )
        stores.append(pltpu.make_async_copy(held.at[rows], out_hbm.at[rows], out_sems.at[part]))
    for copy in loads:
        copy.start()
    for part in range(2):
        loads[2 * part].wait()
        loads[2 * part + 1].wait()
        stores[part].start()
    for copy in stores:
        copy.wait()


def pick_weights(group, gate, up):
    far = pl.BlockSpec(memory_space=pltpu.HBM)
    return pl.pallas_call(
        pick_kernel,
        out_shape=shape(gate.shape, BF16),
        in_specs=[SMEM, far, far],
        out_specs=far,
        scratch_shapes=[
            pltpu.VMEM(gate.shape, BF16),
            pltpu.SemaphoreType.DMA((2, 2)),
            pltpu.SemaphoreType.DMA((2,)),
        ],
        compiler_params=pltpu.CompilerParams(vmem_limit_bytes=63 << 20),
        cost_estimate=pl.CostEstimate(flops=0, bytes_accessed=4 * gate.size, transcendentals=0),
    )(group, gate, up)


def dispatch_kernel(nodes, side, capacity, node_ref, hi_ref, lo_ref, ids_ref, gate_ref, x_ref, c_ref, *out_refs):
    pairs = ids_ref.shape[1]
    sx_refs, sy_refs = out_refs[:nodes], out_refs[nodes:]
    width = sx_refs[0].shape[-1]
    ids = ids_ref[...]
    row = lax.broadcasted_iota(jnp.int32, (pairs, pairs), 0)
    col = lax.broadcasted_iota(jnp.int32, (pairs, pairs), 1)
    earlier = (row < col).astype(BF16)
    slots = lax.broadcasted_iota(jnp.int32, (capacity, pairs), 0)
    for step in range(nodes):
        named = ids == (node_ref[0] ^ step)
        rank = jnp.dot(
            jnp.broadcast_to(jnp.where(named, 1.0, 0.0), (8, pairs)).astype(BF16),
            earlier,
            preferred_element_type=F32,
        )[:1].astype(jnp.int32)
        pick = jnp.where((rank == slots) & named, 1.0, 0.0)
        gate = jnp.sum(pick * gate_ref[...], axis=1, keepdims=True)
        pick = pick.astype(BF16)
        for hi in range(2):
            for lo in range(side):
                block = hi * side + lo
                cols = slice(block * width, (block + 1) * width)
                x_rows = jnp.dot(pick, x_ref[:, cols], preferred_element_type=F32)
                c_rows = jnp.dot(pick, c_ref[:, cols], preferred_element_type=F32)
                sx_refs[step][lo_ref[0] ^ lo, hi_ref[0] ^ hi] = x_rows.astype(BF16)
                sy_refs[step][hi_ref[0] ^ hi, lo_ref[0] ^ lo] = (gate * c_rows).astype(BF16)


def dispatch(node, hi, lo, ids, gates, tokens, cotangent, nodes, side, capacity):
    width = tokens.shape[1] // (2 * side)
    x = shape((side, 2, capacity, width), BF16)
    y = shape((2, side, capacity, width), BF16)
    outs = call(
        functools.partial(dispatch_kernel, nodes, side, capacity),
        4 * nodes * capacity * tokens.size,
        (x,) * nodes + (y,) * nodes,
        (node, hi, lo),
        (ids, gates, tokens, cotangent),
    )
    return outs[:nodes], outs[nodes:]


def owned_rows(own_ref, other_ref, lo, step, pick, nodes, side):
    owner = lo ^ step
    per_core = side // 2
    count = nodes // per_core
    place = (owner % per_core) * count
    rows = []
    for source in range(side):
        own = pick(own_ref, step ^ source, pl.ds(place, count))
        other = pick(other_ref, step ^ source, pl.ds(place, count))
        chosen = jnp.where(owner < per_core, own, other)
        rows.append(chosen.reshape(-1, chosen.shape[-1]))
    return jnp.concatenate(rows, axis=0)


def first_kernel(nodes, side, lo_ref, group_ref, own_ref, other_ref, gate_ref, up_ref, mine_ref, theirs_ref):
    first = group_ref[0] == 0
    half = gate_ref.shape[1] // 2
    for step in range(side):
        pick = lambda ref, source, part: ref[source, part, 0]
        x = owned_rows(own_ref, other_ref, lo_ref[0], step, pick, nodes, side)
        for place, weight_ref in enumerate((gate_ref, up_ref)):
            pre = jnp.dot(x, weight_ref[...], preferred_element_type=F32)
            cols = slice(place * half, (place + 1) * half)
            mine_ref[step, :, cols] = jnp.where(first, pre[:, :half], pre[:, half:])
            theirs_ref[step, :, cols] = jnp.where(first, pre[:, half:], pre[:, :half])


def second_kernel(nodes, side, steps, cuts, lo_ref, own_ref, other_ref, acc_ref, *refs):
    parts = len(cuts) - 1
    weight_refs, out_refs = refs[:parts], refs[parts:]
    for step, out_ref in zip(steps, out_refs):
        pick = lambda ref, source, part: ref[source, part, 1]
        x = owned_rows(own_ref, other_ref, lo_ref[0], step, pick, nodes, side)
        pre = acc_ref[step]
        for start, end, weight_ref in zip(cuts, cuts[1:], weight_refs):
            pre += jnp.dot(x[:, start:end], weight_ref[...], preferred_element_type=F32)
        out_ref[...] = pre.astype(out_ref.dtype)


def partial_first(lo, group, own, other, gate, up, nodes, side):
    chunk = 2 * nodes * own.shape[3]
    acc = shape((side, chunk, gate.shape[1]), F32)
    return call(
        functools.partial(first_kernel, nodes, side),
        4 * side * chunk * gate.size,
        (acc, acc),
        (lo, group),
        (own, other, gate, up),
    )


def partial_second(lo, own, other, acc, weights, cuts, nodes, side, steps, dtype):
    out = shape(acc.shape[1:], dtype)
    return call(
        functools.partial(second_kernel, nodes, side, steps, cuts),
        2 * len(steps) * acc.shape[1] * cuts[-1] * acc.shape[2],
        (out,) * len(steps),
        (lo,),
        (own, other, acc, *weights),
    )


def block_product(nodes, side, hidden_ref, own_ref, other_ref, lo, place):
    hi_step, lo_step = place
    pick = lambda ref, source, part: ref[hi_step, source, part]
    rows = owned_rows(own_ref, other_ref, lo, lo_step, pick, nodes, side)
    return lax.dot_general(
        hidden_ref[...], rows, (((0,), (0,)), ((), ())), preferred_element_type=F32
    )


def near_kernel(nodes, side, lo_ref, group_ref, *refs):
    blocks, (own_ref, other_ref, feedback_ref, done_ref, base_ref) = refs[:-5], refs[-5:]
    half = done_ref.shape[0]
    places = [(h, l) for h in range(2) for l in range(side)]
    sums = []
    for start, count, which in ((0, 2 * side, group_ref[0]), (2 * side, side, 1 - group_ref[0])):
        total = feedback_ref[pl.ds(pl.multiple_of(which * half, half), half), :].astype(F32)
        for block_ref, place in zip(blocks[start : start + count], places):
            total += block_product(nodes, side, block_ref, own_ref, other_ref, lo_ref[0], place)
        sums.append(total)
    done_ref[...] = sums[0].astype(BF16)
    base_ref[...] = sums[1]


def far_kernel(nodes, side, lo_ref, group_ref, *refs):
    blocks, (own_ref, other_ref, done_ref, base_ref, out_ref) = refs[:-5], refs[-5:]
    half = done_ref.shape[0]
    total = base_ref[...]
    for step, block_ref in enumerate(blocks):
        total += block_product(nodes, side, block_ref, own_ref, other_ref, lo_ref[0], (1, step))
    mine, theirs = group_ref[0], 1 - group_ref[0]
    out_ref[pl.ds(pl.multiple_of(mine * half, half), half), :] = done_ref[...]
    out_ref[pl.ds(pl.multiple_of(theirs * half, half), half), :] = total.astype(BF16)


def product(lo, group, first, second, own, other, feedback, nodes, side):
    half, width = first[0].shape[1], own.shape[-1]
    flops = 2 * first[0].size * width
    done, base = call(
        functools.partial(near_kernel, nodes, side),
        3 * side * flops,
        (shape((half, width), BF16), shape((half, width), F32)),
        (lo, group),
        (*first, *second[:side], own, other, feedback),
    )
    return call(
        functools.partial(far_kernel, nodes, side),
        side * flops,
        (shape((2 * half, width), BF16),),
        (lo, group),
        (*second[side:], own, other, done, base),
    )[0]


def local(tokens, cotangent, expert_ids, gate_values, w_gate, w_up, feedback):
    token_count = tokens.shape[0]
    top_count = expert_ids.shape[1]
    nodes, side = lax.axis_size("node"), lax.axis_size("lo")
    capacity = max(2, token_count * top_count // nodes)
    node, hi, lo, group = (
        lax.axis_index(a).astype(jnp.int32)[None] for a in ("node", "hi", "lo", "groups")
    )
    gate_own, up_own = w_gate[0], w_up[0]
    half = gate_own.shape[1] // 2
    width = gate_own.shape[0]
    cuts = (0, width)
    pieces = [pick_weights(group, gate_own, up_own)]
    mine = [swapped(piece, "hi") for piece in pieces]
    theirs = [swapped(piece, "groups") for piece in mine[:-1]]

    if top_count > 1:
        tokens = jnp.repeat(tokens, top_count, axis=0)
        cotangent = jnp.repeat(cotangent, top_count, axis=0)
    send_x, send_y = dispatch(
        node,
        hi,
        lo,
        expert_ids.reshape(1, -1),
        gate_values.reshape(1, -1),
        tokens,
        cotangent,
        nodes,
        side,
        capacity,
    )

    def spread_hidden(pre, came):
        for part in came:
            pre = pre + part.astype(F32)
        hidden = (jax.nn.silu(pre[:, :half]) * pre[:, half:]).astype(BF16)
        across = swapped(hidden, "hi")
        beside = [swapped(hidden, "lo", d) for d in range(1, side)]
        corners = [swapped(across, "lo", d) for d in range(1, side)]
        return [hidden, *beside, across, *corners]

    y = [send_y[0]] + [swapped(send_y[d], "node", d) for d in range(1, nodes)]
    y = [[jnp.stack([part[h, l] for part in y]) for l in range(side)] for h in range(2)]
    x = [[send_x[n][d] for n in range(nodes)] for d in range(side)]
    for d in range(side):
        for n in range(nodes):
            if (n, d) != (0, 0):
                pairs = [(s, s ^ (n * side + d)) for s in range(nodes * side)]
                x[d][n] = lax.ppermute(x[d][n], ("node", "lo"), pairs)
    own_x = jnp.stack([jnp.stack(rows) for rows in x])
    own_x, mine[-1] = lax.optimization_barrier((own_x, mine[-1]))
    other_x = swapped(own_x, "rep")
    acc_mine, acc_theirs = partial_first(lo, group, own_x, other_x, gate_own, up_own, nodes, side)
    theirs.append(swapped(mine[-1], "groups"))
    margs = (lo, own_x, other_x, acc_mine, mine, cuts, nodes, side)
    sends_m = partial_second(*margs, range(1, side), BF16)
    y, mine[-1] = lax.optimization_barrier((y, mine[-1]))
    for h in range(2):
        for l in range(side):
            if (h, l) != (0, 0):
                pairs = [(s, s ^ (h * side + l)) for s in range(2 * side)]
                y[h][l] = lax.ppermute(y[h][l], ("hi", "lo"), pairs)
    came_m = [swapped(send, "lo", d) for d, send in enumerate(sends_m, 1)]
    keep_m = partial_second(*margs, (0,), F32)[0]
    first = spread_hidden(keep_m, came_m)
    own_y = jnp.stack([jnp.stack(row) for row in y])
    other_y = swapped(own_y, "rep")
    first[0], theirs = lax.optimization_barrier((first[0], theirs))
    targs = (lo, own_x, other_x, acc_theirs, theirs, cuts, nodes, side)
    sends_t = partial_second(*targs, range(1, side), BF16)
    came_t = [swapped(send, "lo", d) for d, send in enumerate(sends_t, 1)]
    keep_t = partial_second(*targs, (0,), F32)[0]
    second = spread_hidden(keep_t, came_t)
    return product(lo, group, first, second, own_y, other_y, feedback[0], nodes, side)[None]


def solution(mesh):
    names = ("groups", "node", "hi", "lo", "rep")
    groups, nodes, locals_, reps = (mesh.shape[a] for a in ("groups", "node", "local", "rep"))
    split = Mesh(mesh.devices.reshape(groups, nodes, 2, locals_ // 2, reps), names)
    rows = P(names, None)
    weights = P("node", ("hi", "lo"), "rep")
    return jax.shard_map(
        local,
        mesh=split,
        in_specs=(rows, rows, rows, rows, weights, weights, P("node", "rep", ("hi", "lo"))),
        out_specs=P(("groups", "node"), "rep", ("hi", "lo")),
        check_vma=False,
    )
```

```python
import functools

import jax
import jax.numpy as jnp
from jax import lax
from jax.experimental import pallas as pl
from jax.experimental.pallas import tpu as pltpu
from jax.sharding import Mesh
from jax.sharding import PartitionSpec as P


KERNEL = pltpu.CompilerParams(vmem_limit_bytes=40 << 20)
SMEM = pl.BlockSpec(memory_space=pltpu.SMEM)
WHOLE = pl.BlockSpec()
F32 = jnp.float32
BF16 = jnp.bfloat16


def call(kernel, flops, outs, scalars, arrays):
    size = sum(a.size * a.dtype.itemsize for a in (*arrays, *outs))
    return pl.pallas_call(
        kernel,
        out_shape=outs,
        in_specs=[SMEM] * len(scalars) + [WHOLE] * len(arrays),
        out_specs=(WHOLE,) * len(outs),
        compiler_params=KERNEL,
        cost_estimate=pl.CostEstimate(flops=flops, bytes_accessed=size, transcendentals=0),
    )(*scalars, *arrays)


def shape(dims, dtype):
    return jax.ShapeDtypeStruct(dims, dtype)


def swapped(value, axis, distance=1):
    pairs = [(s, s ^ distance) for s in range(lax.axis_size(axis))]
    return lax.ppermute(value, axis, pairs)


def pick_kernel(group_ref, gate_hbm, up_hbm, out_hbm, held, in_sems, out_sems):
    half = gate_hbm.shape[1] // 2
    count = gate_hbm.shape[0] // 2
    cols = pl.ds(pl.multiple_of(group_ref[0] * half, half), half)
    loads, stores = [], []
    for part in range(2):
        rows = pl.ds(part * count, count)
        for place, source in enumerate((gate_hbm, up_hbm)):
            target = held.at[rows, pl.ds(place * half, half)]
            loads.append(
                pltpu.make_async_copy(source.at[rows, cols], target, in_sems.at[part, place])
            )
        stores.append(pltpu.make_async_copy(held.at[rows], out_hbm.at[rows], out_sems.at[part]))
    for copy in loads:
        copy.start()
    for part in range(2):
        loads[2 * part].wait()
        loads[2 * part + 1].wait()
        stores[part].start()
    for copy in stores:
        copy.wait()


def pick_weights(group, gate, up):
    far = pl.BlockSpec(memory_space=pltpu.HBM)
    return pl.pallas_call(
        pick_kernel,
        out_shape=shape(gate.shape, BF16),
        in_specs=[SMEM, far, far],
        out_specs=far,
        scratch_shapes=[
            pltpu.VMEM(gate.shape, BF16),
            pltpu.SemaphoreType.DMA((2, 2)),
            pltpu.SemaphoreType.DMA((2,)),
        ],
        compiler_params=pltpu.CompilerParams(vmem_limit_bytes=63 << 20),
        cost_estimate=pl.CostEstimate(flops=0, bytes_accessed=4 * gate.size, transcendentals=0),
    )(group, gate, up)


def dispatch_kernel(nodes, side, capacity, node_ref, hi_ref, lo_ref, ids_ref, gate_ref, x_ref, c_ref, *out_refs):
    pairs = ids_ref.shape[1]
    sx_refs, sy_refs = out_refs[:nodes], out_refs[nodes:]
    width = sx_refs[0].shape[-1]
    ids = ids_ref[...]
    row = lax.broadcasted_iota(jnp.int32, (pairs, pairs), 0)
    col = lax.broadcasted_iota(jnp.int32, (pairs, pairs), 1)
    earlier = (row < col).astype(BF16)
    slots = lax.broadcasted_iota(jnp.int32, (capacity, pairs), 0)
    for step in range(nodes):
        named = ids == (node_ref[0] ^ step)
        rank = jnp.dot(
            jnp.broadcast_to(jnp.where(named, 1.0, 0.0), (8, pairs)).astype(BF16),
            earlier,
            preferred_element_type=F32,
        )[:1].astype(jnp.int32)
        pick = jnp.where((rank == slots) & named, 1.0, 0.0)
        gate = jnp.sum(pick * gate_ref[...], axis=1, keepdims=True)
        pick = pick.astype(BF16)
        for hi in range(2):
            for lo in range(side):
                block = hi * side + lo
                cols = slice(block * width, (block + 1) * width)
                x_rows = jnp.dot(pick, x_ref[:, cols], preferred_element_type=F32)
                c_rows = jnp.dot(pick, c_ref[:, cols], preferred_element_type=F32)
                sx_refs[step][lo_ref[0] ^ lo, hi_ref[0] ^ hi] = x_rows.astype(BF16)
                sy_refs[step][hi_ref[0] ^ hi, lo_ref[0] ^ lo] = (gate * c_rows).astype(BF16)


def dispatch(node, hi, lo, ids, gates, tokens, cotangent, nodes, side, capacity):
    width = tokens.shape[1] // (2 * side)
    x = shape((side, 2, capacity, width), BF16)
    y = shape((2, side, capacity, width), BF16)
    outs = call(
        functools.partial(dispatch_kernel, nodes, side, capacity),
        4 * nodes * capacity * tokens.size,
        (x,) * nodes + (y,) * nodes,
        (node, hi, lo),
        (ids, gates, tokens, cotangent),
    )
    return outs[:nodes], outs[nodes:]


def owned_rows(own_ref, other_ref, lo, step, pick, nodes, side):
    owner = lo ^ step
    per_core = side // 2
    count = nodes // per_core
    place = (owner % per_core) * count
    rows = []
    for source in range(side):
        own = pick(own_ref, step ^ source, pl.ds(place, count))
        other = pick(other_ref, step ^ source, pl.ds(place, count))
        chosen = jnp.where(owner < per_core, own, other)
        rows.append(chosen.reshape(-1, chosen.shape[-1]))
    return jnp.concatenate(rows, axis=0)


def first_kernel(nodes, side, lo_ref, group_ref, own_ref, other_ref, gate_ref, up_ref, mine_ref, theirs_ref):
    first = group_ref[0] == 0
    half = gate_ref.shape[1] // 2
    for step in range(side):
        pick = lambda ref, source, part: ref[source, part, 0]
        x = owned_rows(own_ref, other_ref, lo_ref[0], step, pick, nodes, side)
        for place, weight_ref in enumerate((gate_ref, up_ref)):
            pre = jnp.dot(x, weight_ref[...], preferred_element_type=F32)
            cols = slice(place * half, (place + 1) * half)
            mine_ref[step, :, cols] = jnp.where(first, pre[:, :half], pre[:, half:])
            theirs_ref[step, :, cols] = jnp.where(first, pre[:, half:], pre[:, :half])


def second_kernel(nodes, side, steps, cuts, lo_ref, own_ref, other_ref, acc_ref, *refs):
    parts = len(cuts) - 1
    weight_refs, out_refs = refs[:parts], refs[parts:]
    for step, out_ref in zip(steps, out_refs):
        pick = lambda ref, source, part: ref[source, part, 1]
        x = owned_rows(own_ref, other_ref, lo_ref[0], step, pick, nodes, side)
        pre = acc_ref[step]
        for start, end, weight_ref in zip(cuts, cuts[1:], weight_refs):
            pre += jnp.dot(x[:, start:end], weight_ref[...], preferred_element_type=F32)
        out_ref[...] = pre.astype(out_ref.dtype)


def partial_first(lo, group, own, other, gate, up, nodes, side):
    chunk = 2 * nodes * own.shape[3]
    acc = shape((side, chunk, gate.shape[1]), F32)
    return call(
        functools.partial(first_kernel, nodes, side),
        4 * side * chunk * gate.size,
        (acc, acc),
        (lo, group),
        (own, other, gate, up),
    )


def partial_second(lo, own, other, acc, weights, cuts, nodes, side, steps, dtype):
    out = shape(acc.shape[1:], dtype)
    return call(
        functools.partial(second_kernel, nodes, side, steps, cuts),
        2 * len(steps) * acc.shape[1] * cuts[-1] * acc.shape[2],
        (out,) * len(steps),
        (lo,),
        (own, other, acc, *weights),
    )


def block_product(nodes, side, hidden_ref, own_ref, other_ref, lo, place):
    hi_step, lo_step = place
    pick = lambda ref, source, part: ref[hi_step, source, part]
    rows = owned_rows(own_ref, other_ref, lo, lo_step, pick, nodes, side)
    return lax.dot_general(
        hidden_ref[...], rows, (((0,), (0,)), ((), ())), preferred_element_type=F32
    )


def near_kernel(nodes, side, lo_ref, group_ref, *refs):
    blocks, (own_ref, other_ref, feedback_ref, out_hbm, base_ref, done, sem) = refs[:-7], refs[-7:]
    half = done.shape[0]
    places = [(h, l) for h in range(2) for l in range(side)]
    for start, count, which in ((0, 2 * side, group_ref[0]), (2 * side, side, 1 - group_ref[0])):
        rows = pl.ds(pl.multiple_of(which * half, half), half)
        total = feedback_ref[rows, :].astype(F32)
        for block_ref, place in zip(blocks[start : start + count], places):
            total += block_product(nodes, side, block_ref, own_ref, other_ref, lo_ref[0], place)
        if start == 0:
            done[...] = total.astype(BF16)
            copy = pltpu.make_async_copy(done, out_hbm.at[rows], sem)
            copy.start()
        else:
            base_ref[...] = total
    copy.wait()


def far_kernel(nodes, side, lo_ref, group_ref, *refs):
    blocks, (own_ref, other_ref, base_ref, _, out_hbm, done, sem) = refs[:-7], refs[-7:]
    half = done.shape[0]
    total = base_ref[...]
    for step, block_ref in enumerate(blocks):
        total += block_product(nodes, side, block_ref, own_ref, other_ref, lo_ref[0], (1, step))
    done[...] = total.astype(BF16)
    start = pl.multiple_of((1 - group_ref[0]) * half, half)
    copy = pltpu.make_async_copy(done, out_hbm.at[pl.ds(start, half)], sem)
    copy.start()
    copy.wait()


def product(lo, group, first, second, own, other, feedback, nodes, side):
    half, width = first[0].shape[1], own.shape[-1]
    flops = 2 * first[0].size * width
    out = shape((2 * half, width), BF16)
    far = pl.BlockSpec(memory_space=pltpu.HBM)
    scratch = [pltpu.VMEM((half, width), BF16), pltpu.SemaphoreType.DMA]
    estimate = lambda count: pl.CostEstimate(
        flops=count * flops, bytes_accessed=2 * own.size * 2, transcendentals=0
    )
    out, base = pl.pallas_call(
        functools.partial(near_kernel, nodes, side),
        out_shape=(out, shape((half, width), F32)),
        in_specs=[SMEM] * 2 + [WHOLE] * (3 * side + 3),
        out_specs=(far, WHOLE),
        scratch_shapes=scratch,
        compiler_params=KERNEL,
        cost_estimate=estimate(3 * side),
    )(lo, group, *first, *second[:side], own, other, feedback)
    return pl.pallas_call(
        functools.partial(far_kernel, nodes, side),
        out_shape=shape((2 * half, width), BF16),
        in_specs=[SMEM] * 2 + [WHOLE] * (side + 3) + [far],
        out_specs=far,
        scratch_shapes=scratch,
        input_output_aliases={side + 5: 0},
        compiler_params=KERNEL,
        cost_estimate=estimate(side),
    )(lo, group, *second[side:], own, other, base, out)


def local(tokens, cotangent, expert_ids, gate_values, w_gate, w_up, feedback):
    token_count = tokens.shape[0]
    top_count = expert_ids.shape[1]
    nodes, side = lax.axis_size("node"), lax.axis_size("lo")
    capacity = max(2, token_count * top_count // nodes)
    node, hi, lo, group = (
        lax.axis_index(a).astype(jnp.int32)[None] for a in ("node", "hi", "lo", "groups")
    )
    gate_own, up_own = w_gate[0], w_up[0]
    half = gate_own.shape[1] // 2
    width = gate_own.shape[0]
    cuts = (0, width)
    pieces = [pick_weights(group, gate_own, up_own)]
    mine = [swapped(piece, "hi") for piece in pieces]
    theirs = [swapped(piece, "groups") for piece in mine[:-1]]

    if top_count > 1:
        tokens = jnp.repeat(tokens, top_count, axis=0)
        cotangent = jnp.repeat(cotangent, top_count, axis=0)
    send_x, send_y = dispatch(
        node,
        hi,
        lo,
        expert_ids.reshape(1, -1),
        gate_values.reshape(1, -1),
        tokens,
        cotangent,
        nodes,
        side,
        capacity,
    )

    def spread_hidden(pre, came):
        for part in came:
            pre = pre + part.astype(F32)
        hidden = (jax.nn.silu(pre[:, :half]) * pre[:, half:]).astype(BF16)
        across = swapped(hidden, "hi")
        beside = [swapped(hidden, "lo", d) for d in range(1, side)]
        corners = [
            lax.ppermute(hidden, ("hi", "lo"), [(s, s ^ (side + d)) for s in range(2 * side)])
            for d in range(1, side)
        ]
        return [hidden, *beside, across, *corners]

    y = [send_y[0]] + [swapped(send_y[d], "node", d) for d in range(1, nodes)]
    y = [[jnp.stack([part[h, l] for part in y]) for l in range(side)] for h in range(2)]
    x = [[send_x[n][d] for n in range(nodes)] for d in range(side)]
    for d in range(side):
        for n in range(nodes):
            if (n, d) != (0, 0):
                pairs = [(s, s ^ (n * side + d)) for s in range(nodes * side)]
                x[d][n] = lax.ppermute(x[d][n], ("node", "lo"), pairs)
    own_x = jnp.stack([jnp.stack(rows) for rows in x])
    own_x, mine[-1] = lax.optimization_barrier((own_x, mine[-1]))
    other_x = swapped(own_x, "rep")
    acc_mine, acc_theirs = partial_first(lo, group, own_x, other_x, gate_own, up_own, nodes, side)
    theirs.append(swapped(mine[-1], "groups"))
    margs = (lo, own_x, other_x, acc_mine, mine, cuts, nodes, side)
    sends_m = partial_second(*margs, range(1, side), BF16)
    y, mine[-1] = lax.optimization_barrier((y, mine[-1]))
    for h in range(2):
        for l in range(side):
            if (h, l) != (0, 0):
                pairs = [(s, s ^ (h * side + l)) for s in range(2 * side)]
                y[h][l] = lax.ppermute(y[h][l], ("hi", "lo"), pairs)
    came_m = [swapped(send, "lo", d) for d, send in enumerate(sends_m, 1)]
    keep_m = partial_second(*margs, (0,), F32)[0]
    first = spread_hidden(keep_m, came_m)
    targs = (lo, own_x, other_x, acc_theirs, theirs, cuts, nodes, side)
    sends_t = partial_second(*targs, range(1, side), BF16)
    y, sends_t = lax.optimization_barrier((y, sends_t))
    own_y = jnp.stack([jnp.stack(row) for row in y])
    other_y = swapped(own_y, "rep")
    came_t = [swapped(send, "lo", d) for d, send in enumerate(sends_t, 1)]
    keep_t = partial_second(*targs, (0,), F32)[0]
    second = spread_hidden(keep_t, came_t)
    return product(lo, group, first, second, own_y, other_y, feedback[0], nodes, side)[None]


def solution(mesh):
    names = ("groups", "node", "hi", "lo", "rep")
    groups, nodes, locals_, reps = (mesh.shape[a] for a in ("groups", "node", "local", "rep"))
    split = Mesh(mesh.devices.reshape(groups, nodes, 2, locals_ // 2, reps), names)
    rows = P(names, None)
    weights = P("node", ("hi", "lo"), "rep")
    return jax.shard_map(
        local,
        mesh=split,
        in_specs=(rows, rows, rows, rows, weights, weights, P("node", "rep", ("hi", "lo"))),
        out_specs=P(("groups", "node"), "rep", ("hi", "lo")),
        check_vma=False,
    )
```

```python
import functools

import jax
import jax.numpy as jnp
from jax import lax
from jax.experimental import pallas as pl
from jax.experimental.pallas import tpu as pltpu
from jax.sharding import Mesh
from jax.sharding import PartitionSpec as P


KERNEL = pltpu.CompilerParams(vmem_limit_bytes=40 << 20)
SMEM = pl.BlockSpec(memory_space=pltpu.SMEM)
WHOLE = pl.BlockSpec()
F32 = jnp.float32
BF16 = jnp.bfloat16


def call(kernel, flops, outs, scalars, arrays):
    size = sum(a.size * a.dtype.itemsize for a in (*arrays, *outs))
    return pl.pallas_call(
        kernel,
        out_shape=outs,
        in_specs=[SMEM] * len(scalars) + [WHOLE] * len(arrays),
        out_specs=(WHOLE,) * len(outs),
        compiler_params=KERNEL,
        cost_estimate=pl.CostEstimate(flops=flops, bytes_accessed=size, transcendentals=0),
    )(*scalars, *arrays)


def shape(dims, dtype):
    return jax.ShapeDtypeStruct(dims, dtype)


def swapped(value, axis, distance=1):
    pairs = [(s, s ^ distance) for s in range(lax.axis_size(axis))]
    return lax.ppermute(value, axis, pairs)


def pick_kernel(group_ref, gate_hbm, up_hbm, out_hbm, held, in_sems, out_sems):
    half = gate_hbm.shape[1] // 2
    count = gate_hbm.shape[0] // 2
    cols = pl.ds(pl.multiple_of(group_ref[0] * half, half), half)
    loads, stores = [], []
    for part in range(2):
        rows = pl.ds(part * count, count)
        for place, source in enumerate((gate_hbm, up_hbm)):
            target = held.at[rows, pl.ds(place * half, half)]
            loads.append(
                pltpu.make_async_copy(source.at[rows, cols], target, in_sems.at[part, place])
            )
        stores.append(pltpu.make_async_copy(held.at[rows], out_hbm.at[rows], out_sems.at[part]))
    for copy in loads:
        copy.start()
    for part in range(2):
        loads[2 * part].wait()
        loads[2 * part + 1].wait()
        stores[part].start()
    for copy in stores:
        copy.wait()


def pick_weights(group, gate, up):
    far = pl.BlockSpec(memory_space=pltpu.HBM)
    return pl.pallas_call(
        pick_kernel,
        out_shape=shape(gate.shape, BF16),
        in_specs=[SMEM, far, far],
        out_specs=far,
        scratch_shapes=[
            pltpu.VMEM(gate.shape, BF16),
            pltpu.SemaphoreType.DMA((2, 2)),
            pltpu.SemaphoreType.DMA((2,)),
        ],
        compiler_params=pltpu.CompilerParams(vmem_limit_bytes=63 << 20),
        cost_estimate=pl.CostEstimate(flops=0, bytes_accessed=4 * gate.size, transcendentals=0),
    )(group, gate, up)


def dispatch_kernel(nodes, side, capacity, node_ref, hi_ref, lo_ref, ids_ref, gate_ref, x_ref, c_ref, *out_refs):
    pairs = ids_ref.shape[1]
    sx_refs, sy_refs = out_refs[:nodes], out_refs[nodes:]
    width = sx_refs[0].shape[-1]
    ids = ids_ref[...]
    row = lax.broadcasted_iota(jnp.int32, (pairs, pairs), 0)
    col = lax.broadcasted_iota(jnp.int32, (pairs, pairs), 1)
    earlier = (row < col).astype(BF16)
    slots = lax.broadcasted_iota(jnp.int32, (capacity, pairs), 0)
    for step in range(nodes):
        named = ids == (node_ref[0] ^ step)
        rank = jnp.dot(
            jnp.broadcast_to(jnp.where(named, 1.0, 0.0), (8, pairs)).astype(BF16),
            earlier,
            preferred_element_type=F32,
        )[:1].astype(jnp.int32)
        pick = jnp.where((rank == slots) & named, 1.0, 0.0)
        gate = jnp.sum(pick * gate_ref[...], axis=1, keepdims=True)
        pick = pick.astype(BF16)
        for hi in range(2):
            for lo in range(side):
                block = hi * side + lo
                cols = slice(block * width, (block + 1) * width)
                x_rows = jnp.dot(pick, x_ref[:, cols], preferred_element_type=F32)
                c_rows = jnp.dot(pick, c_ref[:, cols], preferred_element_type=F32)
                sx_refs[step][lo_ref[0] ^ lo, hi_ref[0] ^ hi] = x_rows.astype(BF16)
                sy_refs[step][hi_ref[0] ^ hi, lo_ref[0] ^ lo] = (gate * c_rows).astype(BF16)


def dispatch(node, hi, lo, ids, gates, tokens, cotangent, nodes, side, capacity):
    width = tokens.shape[1] // (2 * side)
    x = shape((side, 2, capacity, width), BF16)
    y = shape((2, side, capacity, width), BF16)
    outs = call(
        functools.partial(dispatch_kernel, nodes, side, capacity),
        4 * nodes * capacity * tokens.size,
        (x,) * nodes + (y,) * nodes,
        (node, hi, lo),
        (ids, gates, tokens, cotangent),
    )
    return outs[:nodes], outs[nodes:]


def owned_rows(own_ref, other_ref, lo, step, pick, nodes, side):
    owner = lo ^ step
    per_core = side // 2
    count = nodes // per_core
    place = (owner % per_core) * count
    rows = []
    for source in range(side):
        own = pick(own_ref, step ^ source, pl.ds(place, count))
        other = pick(other_ref, step ^ source, pl.ds(place, count))
        chosen = jnp.where(owner < per_core, own, other)
        rows.append(chosen.reshape(-1, chosen.shape[-1]))
    return jnp.concatenate(rows, axis=0)


def first_kernel(nodes, side, lo_ref, group_ref, own_ref, other_ref, gate_ref, up_ref, mine_ref, theirs_ref):
    first = group_ref[0] == 0
    half = gate_ref.shape[1] // 2
    for step in range(side):
        pick = lambda ref, source, part: ref[source, part, 0]
        x = owned_rows(own_ref, other_ref, lo_ref[0], step, pick, nodes, side)
        for place, weight_ref in enumerate((gate_ref, up_ref)):
            pre = jnp.dot(x, weight_ref[...], preferred_element_type=F32)
            cols = slice(place * half, (place + 1) * half)
            mine_ref[step, :, cols] = jnp.where(first, pre[:, :half], pre[:, half:])
            theirs_ref[step, :, cols] = jnp.where(first, pre[:, half:], pre[:, :half])


def second_kernel(nodes, side, steps, cuts, lo_ref, own_ref, other_ref, acc_ref, *refs):
    parts = len(cuts) - 1
    weight_refs, out_refs = refs[:parts], refs[parts:]
    for step, out_ref in zip(steps, out_refs):
        pick = lambda ref, source, part: ref[source, part, 1]
        x = owned_rows(own_ref, other_ref, lo_ref[0], step, pick, nodes, side)
        pre = acc_ref[step]
        for start, end, weight_ref in zip(cuts, cuts[1:], weight_refs):
            pre += jnp.dot(x[:, start:end], weight_ref[...], preferred_element_type=F32)
        out_ref[...] = pre.astype(out_ref.dtype)


def partial_first(lo, group, own, other, gate, up, nodes, side):
    chunk = 2 * nodes * own.shape[3]
    acc = shape((side, chunk, gate.shape[1]), F32)
    return call(
        functools.partial(first_kernel, nodes, side),
        4 * side * chunk * gate.size,
        (acc, acc),
        (lo, group),
        (own, other, gate, up),
    )


def partial_second(lo, own, other, acc, weights, cuts, nodes, side, steps, dtype):
    out = shape(acc.shape[1:], dtype)
    return call(
        functools.partial(second_kernel, nodes, side, steps, cuts),
        2 * len(steps) * acc.shape[1] * cuts[-1] * acc.shape[2],
        (out,) * len(steps),
        (lo,),
        (own, other, acc, *weights),
    )


def block_product(nodes, side, hidden_ref, own_ref, other_ref, lo, place):
    hi_step, lo_step = place
    pick = lambda ref, source, part: ref[hi_step, source, part]
    rows = owned_rows(own_ref, other_ref, lo, lo_step, pick, nodes, side)
    return lax.dot_general(
        hidden_ref[...], rows, (((0,), (0,)), ((), ())), preferred_element_type=F32
    )


def near_kernel(nodes, side, lo_ref, group_ref, *refs):
    blocks, (own_ref, other_ref, feedback_ref, out_hbm, base_ref, done, sem) = refs[:-7], refs[-7:]
    half = done.shape[0]
    places = [(h, l) for h in range(2) for l in range(side)]
    for start, count, which in ((0, 2 * side, group_ref[0]), (2 * side, side, 1 - group_ref[0])):
        rows = pl.ds(pl.multiple_of(which * half, half), half)
        total = feedback_ref[rows, :].astype(F32)
        for block_ref, place in zip(blocks[start : start + count], places):
            total += block_product(nodes, side, block_ref, own_ref, other_ref, lo_ref[0], place)
        if start == 0:
            done[...] = total.astype(BF16)
            copy = pltpu.make_async_copy(done, out_hbm.at[rows], sem)
            copy.start()
        else:
            base_ref[...] = total
    copy.wait()


def far_kernel(nodes, side, lo_ref, group_ref, *refs):
    blocks, (own_ref, other_ref, base_ref, _, out_hbm, done, sem) = refs[:-7], refs[-7:]
    half = done.shape[0]
    total = base_ref[...]
    for step, block_ref in enumerate(blocks):
        total += block_product(nodes, side, block_ref, own_ref, other_ref, lo_ref[0], (1, step))
    done[...] = total.astype(BF16)
    start = pl.multiple_of((1 - group_ref[0]) * half, half)
    copy = pltpu.make_async_copy(done, out_hbm.at[pl.ds(start, half)], sem)
    copy.start()
    copy.wait()


def product(lo, group, first, second, own, other, feedback, nodes, side):
    half, width = first[0].shape[1], own.shape[-1]
    flops = 2 * first[0].size * width
    out = shape((2 * half, width), BF16)
    far = pl.BlockSpec(memory_space=pltpu.HBM)
    scratch = [pltpu.VMEM((half, width), BF16), pltpu.SemaphoreType.DMA]
    estimate = lambda count: pl.CostEstimate(
        flops=count * flops, bytes_accessed=2 * own.size * 2, transcendentals=0
    )
    out, base = pl.pallas_call(
        functools.partial(near_kernel, nodes, side),
        out_shape=(out, shape((half, width), F32)),
        in_specs=[SMEM] * 2 + [WHOLE] * (3 * side + 3),
        out_specs=(far, WHOLE),
        scratch_shapes=scratch,
        compiler_params=KERNEL,
        cost_estimate=estimate(3 * side),
    )(lo, group, *first, *second[:side], own, other, feedback)
    return pl.pallas_call(
        functools.partial(far_kernel, nodes, side),
        out_shape=shape((2 * half, width), BF16),
        in_specs=[SMEM] * 2 + [WHOLE] * (side + 3) + [far],
        out_specs=far,
        scratch_shapes=scratch,
        input_output_aliases={side + 5: 0},
        compiler_params=KERNEL,
        cost_estimate=estimate(side),
    )(lo, group, *second[side:], own, other, base, out)


def local(tokens, cotangent, expert_ids, gate_values, w_gate, w_up, feedback):
    token_count = tokens.shape[0]
    top_count = expert_ids.shape[1]
    nodes, side = lax.axis_size("node"), lax.axis_size("lo")
    capacity = max(2, token_count * top_count // nodes)
    node, hi, lo, group = (
        lax.axis_index(a).astype(jnp.int32)[None] for a in ("node", "hi", "lo", "groups")
    )
    gate_own, up_own = w_gate[0], w_up[0]
    half = gate_own.shape[1] // 2
    width = gate_own.shape[0]
    cuts = (0, width)
    pieces = [pick_weights(group, gate_own, up_own)]
    mine = [swapped(piece, "hi") for piece in pieces]
    theirs = [swapped(piece, "groups") for piece in mine[:-1]]

    if top_count > 1:
        tokens = jnp.repeat(tokens, top_count, axis=0)
        cotangent = jnp.repeat(cotangent, top_count, axis=0)
    send_x, send_y = dispatch(
        node,
        hi,
        lo,
        expert_ids.reshape(1, -1),
        gate_values.reshape(1, -1),
        tokens,
        cotangent,
        nodes,
        side,
        capacity,
    )

    def spread_hidden(pre, came):
        for part in came:
            pre = pre + part.astype(F32)
        hidden = (jax.nn.silu(pre[:, :half]) * pre[:, half:]).astype(BF16)
        across = swapped(hidden, "hi")
        beside = [swapped(hidden, "lo", d) for d in range(1, side)]
        corners = [swapped(across, "lo", d) for d in range(1, side)]
        return [hidden, *beside, across, *corners]

    y = [send_y[0]] + [swapped(send_y[d], "node", d) for d in range(1, nodes)]
    y = [[jnp.stack([part[h, l] for part in y]) for l in range(side)] for h in range(2)]
    x = [[send_x[n][d] for n in range(nodes)] for d in range(side)]
    for d in range(side):
        for n in range(nodes):
            if (n, d) != (0, 0):
                pairs = [(s, s ^ (n * side + d)) for s in range(nodes * side)]
                x[d][n] = lax.ppermute(x[d][n], ("node", "lo"), pairs)
    own_x = jnp.stack([jnp.stack(rows) for rows in x])
    own_x, mine[-1] = lax.optimization_barrier((own_x, mine[-1]))
    other_x = swapped(own_x, "rep")
    acc_mine, acc_theirs = partial_first(lo, group, own_x, other_x, gate_own, up_own, nodes, side)
    theirs.append(swapped(mine[-1], "groups"))
    margs = (lo, own_x, other_x, acc_mine, mine, cuts, nodes, side)
    sends_m = partial_second(*margs, range(1, side), BF16)
    y, mine[-1] = lax.optimization_barrier((y, mine[-1]))
    for h in range(2):
        for l in range(side):
            if (h, l) != (0, 0):
                pairs = [(s, s ^ (h * side + l)) for s in range(2 * side)]
                y[h][l] = lax.ppermute(y[h][l], ("hi", "lo"), pairs)
    came_m = [swapped(send, "lo", d) for d, send in enumerate(sends_m, 1)]
    keep_m = partial_second(*margs, (0,), F32)[0]
    first = spread_hidden(keep_m, came_m)
    own_y = jnp.stack([jnp.stack(row) for row in y])
    other_y = swapped(own_y, "rep")
    first[0], theirs = lax.optimization_barrier((first[0], theirs))
    targs = (lo, own_x, other_x, acc_theirs, theirs, cuts, nodes, side)
    sends_t = partial_second(*targs, range(1, side), BF16)
    came_t = [swapped(send, "lo", d) for d, send in enumerate(sends_t, 1)]
    keep_t = partial_second(*targs, (0,), F32)[0]
    second = spread_hidden(keep_t, came_t)
    return product(lo, group, first, second, own_y, other_y, feedback[0], nodes, side)[None]


def solution(mesh):
    names = ("groups", "node", "hi", "lo", "rep")
    groups, nodes, locals_, reps = (mesh.shape[a] for a in ("groups", "node", "local", "rep"))
    split = Mesh(mesh.devices.reshape(groups, nodes, 2, locals_ // 2, reps), names)
    rows = P(names, None)
    weights = P("node", ("hi", "lo"), "rep")
    return jax.shard_map(
        local,
        mesh=split,
        in_specs=(rows, rows, rows, rows, weights, weights, P("node", "rep", ("hi", "lo"))),
        out_specs=P(("groups", "node"), "rep", ("hi", "lo")),
        check_vma=False,
    )
```
